256 devices in a mesh: patch: 32 (over x, z), freq: 8 (over y, core).
Axes of the slice: x: 4, y: 4, z: 8, core: 2. Of those that a mesh axis runs over, the one named last changes fastest.
Arguments:
- traces: bfloat16 [262144, 2048], P(('patch', 'freq')), may hold values from -6 to 6
- routes: int32 [262144, 1], P(('patch', 'freq')), may hold values from 0 to 31; in each aligned block of 1024 rows (0 to 1023, 1024 to 2047, ...) at most 96 rows name the same one
- cells: int32 [262144], P(('patch', 'freq')), may hold values from 0 to 65535
- band_bins: int32 [16], P('freq'), may hold values from 8 to 1023, as said below
- spectral_weight: float32 [16, 2097152], P('freq', 'patch'), may hold values from 0.1 to 1
Outputs:
- interpolated: float32 [2, 16, 2097152], P(None, 'freq', 'patch')
The draws below stay inside these ranges and needn't reach their ends.
Inputs may be any that keep to these rules, and one draw needn't show every extreme that they name: `band_bins`: distinct and rising frequency bin numbers; the lowest and the highest bin of the range are always in the band.
All inputs are finite; a program needn't handle non-finite values.
Results may differ from the reference program's by a relative error of at most 0.003.
Values may be sent and summed in bfloat16 or wider, within the bound.
A program may use at most 256 MiB of HBM per device.

```python
import math
import jax
import jax.numpy as jnp
import numpy as np
from jax import lax

NT = 2048
SIDE = 16
CELLS = 65536
TR_DEV = 1024
ITERS = 2
FREQS = 16
TRACES = 262144
CAP = 96
N_PATCH = 32


def draw_band_bins(key, part):
    key = jax.random.fold_in(key, 11)
    shuffled = jax.random.permutation(key, NT // 2 - 10)
    inner = shuffled[:FREQS - 2] + 9
    ends = jnp.array([8, NT // 2 - 1], dtype=jnp.int32)
    return jnp.sort(jnp.concatenate([inner.astype(jnp.int32), ends])).astype(jnp.int32)


def place_ends(values, own_key, low, high):
    spot = [jax.random.randint(jax.random.fold_in(own_key, axis), (), 0, length) for axis, length in enumerate(values.shape)]
    main_axis = values.shape.index(max(values.shape))
    beside = spot[:main_axis] + [(spot[main_axis] + 1) % values.shape[main_axis]] + spot[main_axis + 1:]
    return values.at[tuple(spot)].set(low).at[tuple(beside)].set(high)


def levels(key, dims, pieces, low, high):
    def one(axis_at, parts):
        steps = jax.random.uniform(jax.random.fold_in(jax.random.fold_in(key, 6), axis_at), (parts,), jnp.float32, low / len(pieces), high / len(pieces))
        return jnp.repeat(jnp.exp(steps), dims[axis_at] // parts).reshape((-1,) + (1,) * (len(dims) - axis_at - 1))

    factor_of = one(*pieces[0])
    for cut in pieces[1:]:
        factor_of = factor_of * one(*cut)
    return factor_of


def deal_out(key, own, number, rows, count, top, reach, lean):
    order = jax.random.permutation(key, count)
    crowded, usual = load_shares(count, rows * top, reach, lean, True), load_shares(count, rows * top, reach, lean, False)
    places = jnp.arange(count)

    def named(sizes, offset_by):
        used = int((sizes > 0).sum())
        fixed = max(1, used // 4)
        shifted = fixed + (places - fixed + offset_by * (used - fixed)) % max(1, count - fixed)
        return jnp.zeros((count,), jnp.int32).at[order[jnp.where(places < fixed, places, shifted)]].set(jnp.asarray(sizes, jnp.int32))

    sizes = jnp.where(number % 4 == 0, named(crowded, number // 4), named(usual, number - number // 4 - 1))
    mixed = jax.random.permutation(jax.random.fold_in(own, 3), count)
    source_of, taker = mixed[0:count // 2 * 2:2], mixed[1:count // 2 * 2:2]
    room = jnp.minimum(sizes[source_of] - 1, reach - sizes[taker]) // 2
    room = jnp.where((source_of == order[0]) | (taker == order[0]) | (sizes[taker] == 0), 0, jnp.maximum(room, 0))
    shifted = jax.random.randint(jax.random.fold_in(own, 4), (count // 2,), 0, 1 << 20) % (room + 1)
    sizes = sizes.at[source_of].add(-shifted).at[taker].add(shifted)
    items = jnp.searchsorted(jnp.cumsum(sizes), jnp.arange(rows * top), side="right").astype(jnp.int32)
    listing = items.reshape(top, rows).T
    listing = listing[jax.random.permutation(jax.random.fold_in(own, 1), rows)]
    offset_by = jax.random.randint(jax.random.fold_in(own, 2), (rows, 1), 0, top)
    return jnp.take_along_axis(listing, (jnp.arange(top)[None, :] + offset_by) % top, axis=1)


def load_shares(amount, total, reach, skew, full):
    portions = [(1 << 20) // math.isqrt(standing ** skew) + 1 for standing in range(1, amount + 1)]
    largest = reach if full else min(reach, max(-(-total // amount), total * portions[0] // sum(portions)))
    least = 1 if total - largest >= amount - 1 else 0
    given, surplus = [largest] + [least] * (amount - 1), total - largest - least * (amount - 1)
    while surplus > 0:
        candidates = [i for i in range(1, amount) if given[i] < largest] or [i for i in range(1, amount) if given[i] < reach]
        whole, budget = sum([portions[i] for i in candidates]), surplus
        for i in candidates:
            addition = min(reach - given[i], max(1, budget * portions[i] // whole), surplus)
            given[i] = given[i] + addition
            surplus = surplus - addition
    return np.array(given)


def normal_values(own_key, extent, deviation, bound, shards=(), held_as=jnp.bfloat16):
    values = jax.random.normal(own_key, extent, jnp.float32) * deviation
    if len(shards) > 0:
        values = levels(own_key, extent, shards, -0.22, 0.18) * values
    return jnp.clip(values, min=-bound, max=bound).astype(held_as)


def setup_inputs(seed: int = 0) -> dict:
    key_of = jax.random.split(jax.random.key(seed), 6)
    traces = normal_values(key_of[0], (TRACES, NT), 1.0, 6.0, ((0, 256),))
    routes_keys = jax.random.split(jax.random.fold_in(key_of[1], 1), TRACES // TR_DEV)
    routes_turns = jax.random.permutation(jax.random.fold_in(key_of[1], 3), TRACES // TR_DEV)
    routes = jax.vmap(lambda own, number: deal_out(jax.random.fold_in(key_of[1], 2), own, number, TR_DEV, N_PATCH, 1, CAP, 2))(routes_keys, routes_turns).reshape((TRACES, 1))
    cells = place_ends(jax.random.randint(key_of[2], (TRACES,), 0, CELLS), jax.random.fold_in(key_of[2], 1), 0, CELLS - 1).astype(jnp.int32)
    band_bins = draw_band_bins(jax.random.fold_in(key_of[5], 71), 0)
    spectral_weight = jnp.clip(jnp.exp(math.log(1.0) - 2.3025851 * jax.random.uniform(key_of[4], (FREQS, N_PATCH * CELLS), jnp.float32) ** levels(key_of[4], (FREQS, N_PATCH * CELLS), ((0, 8), (1, 32)), -0.2, 0.2)), 0.1, 1.0)
    return dict(traces=traces, routes=routes, cells=cells, band_bins=band_bins, spectral_weight=spectral_weight)


EPS = 1e-06
DAMPING = 0.1

def spectral_table(bins, sample_count):
    sample_index = jnp.arange(sample_count, dtype=jnp.int32)
    phase = bins.astype(jnp.int32)[:, None] * sample_index[None, :] % sample_count
    angle = 2.0 * math.pi / sample_count * phase.astype(jnp.float32)
    factor = 1.0 / math.sqrt(sample_count)
    return jnp.concatenate([jnp.cos(angle) * factor, -jnp.sin(angle) * factor], 0).astype(jnp.bfloat16)

def solve_patch(items):
    binned, counts, weight = items
    shape_four = (FREQS, SIDE, SIDE, SIDE, SIDE)
    cell_axes = (1, 2, 3, 4)
    weight = weight.reshape(shape_four)
    counts = counts.reshape(shape_four[1:])

    def forward(field):
        return jnp.fft.fftn(field, axes=cell_axes, norm='ortho')

    def inverse(field):
        return jnp.fft.ifftn(field, axes=cell_axes, norm='ortho')

    def column(values):
        return values.reshape(FREQS, 1, 1, 1, 1)
    field = (binned[0] + 1j * binned[1]).reshape(shape_four)
    right_side = weight * forward(field)
    estimate = jnp.zeros_like(right_side)
    residual = right_side
    direction = right_side
    norm_now = lax.optimization_barrier(jnp.sum(jnp.abs(residual) ** 2, axis=cell_axes))
    for step in range(ITERS):
        image = weight * forward(counts * inverse(weight * direction)) + DAMPING * direction
        curvature = jnp.real(lax.optimization_barrier(jnp.sum(jnp.conj(direction) * image, axis=cell_axes)))
        alpha = column(norm_now / (curvature + EPS))
        estimate = estimate + alpha * direction
        residual = residual - alpha * image
        norm_next = lax.optimization_barrier(jnp.sum(jnp.abs(residual) ** 2, axis=cell_axes))
        direction = residual + column(norm_next / (norm_now + EPS)) * direction
        norm_now = norm_next
    model_field = inverse(weight * estimate)
    return jnp.stack([jnp.real(model_field), jnp.imag(model_field)]).reshape(2, FREQS, CELLS)

def reference(traces, routes, cells, band_bins, spectral_weight):
    basis = spectral_table(band_bins, NT)
    spectra = jnp.dot(basis, traces.T, preferred_element_type=jnp.float32)
    flat_index = (routes[:, 0].astype(jnp.int32) * CELLS + cells.astype(jnp.int32)).astype(jnp.int32)
    binned = jnp.zeros((2 * FREQS, N_PATCH * CELLS), jnp.float32).at[:, flat_index].add(spectra)
    counts = jnp.zeros((N_PATCH * CELLS,), jnp.float32).at[flat_index].add(jnp.float32(1.0))
    binned = binned.reshape(2, FREQS, N_PATCH, CELLS).transpose(2, 0, 1, 3)
    counts = counts.reshape(N_PATCH, CELLS)
    weight = spectral_weight.reshape(FREQS, N_PATCH, CELLS).transpose(1, 0, 2)
    result = lax.map(solve_patch, (binned, counts, weight))
    return result.transpose(1, 2, 0, 3).reshape(2, FREQS, N_PATCH * CELLS)
```

```python
import functools, math
import jax, jax.numpy as jnp
import ml_dtypes
import numpy as np
from jax import lax
from jax.experimental import pallas as pl
from jax.experimental.pallas import tpu as pltpu
F32=jnp.float32; BF=jnp.bfloat16
NTD=(((1,),(1,)),((),()))

def cosine(phase, n):
    quad = (phase + n // 8) // (n // 4)
    rest = (phase - quad * (n // 4)).astype(F32) * (2.0 * math.pi / n)
    sq = rest * rest
    c = 1.0 + sq * (-0.5 + sq * (1.0/24 + sq * (-1.0/720 + sq * (1.0/40320))))
    s = rest * (1.0 + sq * (-1.0/6 + sq * (1.0/120 + sq * (-1.0/5040))))
    odd = (quad & 1) == 1
    val = jnp.where(odd, s, c)
    neg = ((quad + 1) & 2) == 2
    return jnp.where(neg, -val, val)

def make_basis(bins_ref, nt):
    row = lax.broadcasted_iota(jnp.int32, (32, 128), 0)
    which = (row // 4) * 2 + (row & 1)
    k = jnp.zeros((32, 128), jnp.int32)
    for i in range(16):
        k = jnp.where(which == i, bins_ref[i], k)
    part = (row // 2) & 1
    t = lax.broadcasted_iota(jnp.int32, (32, nt), 1)
    kk = jnp.concatenate([k] * (nt // 128), axis=1)
    pp = jnp.concatenate([part] * (nt // 128), axis=1)
    phase = (kk * t + pp * (nt // 4)) & (nt - 1)
    return (cosine(phase, nt) * (1.0 / math.sqrt(nt))).astype(BF)

def routing(route, cell):
    rows = route.shape[1]
    member = (lax.broadcasted_iota(jnp.int32, (32, rows), 0) == route).astype(F32)
    tri = (lax.broadcasted_iota(jnp.int32, (128, 128), 0) < lax.broadcasted_iota(jnp.int32, (128, 128), 1)).astype(F32).astype(BF)
    pieces = [member[:, 128*i:128*i+128] for i in range(rows // 128)]
    inside = jnp.dot(jnp.concatenate(pieces, axis=0).astype(BF), tri, preferred_element_type=F32)
    offset = jnp.zeros((32, 1), F32)
    before = []
    for i, piece in enumerate(pieces):
        before.append(inside[32*i:32*i+32] + offset)
        offset = offset + jnp.sum(piece, axis=1, keepdims=True)
    rank = jnp.sum(member * jnp.concatenate(before, axis=1), axis=0, keepdims=True).astype(jnp.int32)
    return route * 32 + (rank & 31), rank >> 5

def stack_rows(spectra, third, cell):
    rows = spectra.shape[1]
    out = [jnp.where(third == q, spectra, 0.0) for q in range(3)]
    r = lax.broadcasted_iota(jnp.int32, (32, rows), 0)
    high = ((cell >> 8) + 1).astype(F32)
    low = (cell & 255).astype(F32)
    code = jnp.where((r & 4) == 0, high, low)
    out.append(jnp.where((r >> 3) == third, code, 0.0))
    return jnp.concatenate(out, axis=0).astype(BF)

def one_hot_rows(key):
    rows = key.shape[1]
    return jnp.where(lax.broadcasted_iota(jnp.int32, (1024, rows), 0) == key, 1.0, 0.0).astype(BF)

def write_messages(packed, msg_ref):
    lane = lax.broadcasted_iota(jnp.int32, (32, 128), 1) >> 5
    for cb in range(8):
        groups = [packed[32*g:32*g+32, 128*cb:128*cb+128] for g in range(4)]
        for pm in range(4):
            out = jnp.zeros((32, 128), F32)
            for g in range(4):
                piece = groups[g]
                shift = (32 * (g - pm)) % 128
                if shift:
                    piece = pltpu.roll(piece, shift, 1)
                out = jnp.where(lane == g, piece, out)
            msg_ref[4*cb+pm] = out.astype(BF)

def prepare_kernel(bins_ref, traces_ref, route_ref, cell_ref, msg_ref):
    basis = make_basis(bins_ref, traces_ref.shape[1])
    key, third = routing(route_ref[...], cell_ref[...])
    spectra = lax.dot_general(basis, traces_ref[...], NTD, preferred_element_type=F32)
    stacked = stack_rows(spectra, third, cell_ref[...])
    packed = lax.dot_general(stacked, one_hot_rows(key), NTD, preferred_element_type=F32)
    write_messages(packed, msg_ref)

def regroup_kernel(msg_ref, val_ref, cell_ref):
    lane = lax.broadcasted_iota(jnp.int32, (32, 128), 1) >> 5
    lane8 = lane[:8]
    sub = lax.broadcasted_iota(jnp.int32, (8, 128), 0)
    dense, codes = [], []
    for h in range(8):
        msgs = [msg_ref[4*h+i].astype(F32) for i in range(4)]
        for k in range(3):
            last = pltpu.roll(msgs[3], 96 - 32*k, 1)
            dense.append(jnp.where(lane < 3, msgs[k], last))
            out = msgs[3][8*k:8*k+8]
            for q in range(3):
                out = jnp.where(lane8 == q, pltpu.roll(msgs[k][8*q:8*q+8], 32 + 32*q, 1), out)
            codes.append(out)
    for f in range(8):
        tiles = []
        for pair in range(12):
            a = dense[2*pair][8*(f//2):8*(f//2)+8]
            b = dense[2*pair+1][8*(f//2):8*(f//2)+8]
            if f % 2 == 0:
                b = pltpu.roll(b, 4, 0)
            else:
                a = pltpu.roll(a, 4, 0)
            tiles.append(jnp.where(sub < 4, a, b))
        val_ref[f] = jnp.concatenate(tiles, axis=0).astype(BF)
    out = []
    for cg in range(6):
        t = codes[4*cg]
        for i in range(1, 4):
            t = jnp.where((sub & 3) == i, codes[4*cg+i], t)
        out.append(t)
    cell_ref[...] = jnp.concatenate(out, axis=0).astype(BF)
from jax.sharding import PartitionSpec as P
SIDE=16; ITERS=2; EPS=1e-6; DAMPING=0.1

def kernel_table():
    flat = np.arange(256)
    up, lo = flat // 16, flat % 16
    phase = (up[:, None]*up[None, :] + lo[:, None]*lo[None, :]) % 16
    ang = 2.0*np.pi/16*phase
    kr = np.cos(ang)/16; ki = -np.sin(ang)/16
    a = np.block([[kr, -ki], [ki, kr]])
    b = np.block([[kr, ki], [-ki, kr]])
    def parts(m):
        hi = m.astype(ml_dtypes.bfloat16)
        lo = (m - hi.astype(np.float64)).astype(ml_dtypes.bfloat16)
        return hi, lo
    ah, al = parts(a); bh, bl = parts(b)
    return np.stack([ah, al, bh, bl])

def bin_step(vals, codes, cg, iota, comps=4):
    u = jnp.concatenate([codes[8*cg+i:8*cg+i+1] for i in range(4)], axis=1)
    l = jnp.concatenate([codes[8*cg+4+i:8*cg+5+i] for i in range(4)], axis=1)
    mask = (iota + 1.0) == u
    rhs = jnp.where(iota == l, 1.0, 0.0).astype(BF)
    rows = []
    for c in range(comps):
        v = jnp.concatenate([vals[4*(4*cg+i)+c:4*(4*cg+i)+c+1] for i in range(4)], axis=1)
        rows.append(jnp.where(mask, v, 0.0).astype(BF))
    rows.append(jnp.where(mask, 1.0, 0.0).astype(BF))
    return jnp.concatenate(rows, axis=0), rhs

def split(x):
    hi = x.astype(BF)
    return hi, (x - hi.astype(F32)).astype(BF)

def swap(x):
    return jnp.concatenate([jnp.concatenate([x[:256,:256], x[256:,:256]], axis=1),
                            jnp.concatenate([x[:256,256:], x[256:,256:]], axis=1)], axis=0)

def solve_kernel(val_ref, code_ref, w_ref, tab_ref, out_ref, acc_ref):
    acc_ref[...] = jnp.zeros_like(acc_ref)
    @pl.loop(0, 8)
    def _(g):
        vals = val_ref[g].astype(F32)
        codes = code_ref[g].astype(F32)
        iota = lax.broadcasted_iota(jnp.int32, (256, 512), 0).astype(F32)
        for cg in range(6):
            lhs, rhs = bin_step(vals, codes, cg, iota)
            acc_ref[...] += lax.dot_general(lhs, rhs, NTD, preferred_element_type=F32)
    def left(x, which):
        hi, lo = split(x)
        m, ml = tab_ref[2*which], tab_ref[2*which+1]
        d = functools.partial(jnp.dot, preferred_element_type=F32)
        return d(m, hi) + d(m, lo) + d(ml, hi)
    def right(x, which):
        hi, lo = split(x)
        m, ml = tab_ref[2*which], tab_ref[2*which+1]
        d = functools.partial(jnp.dot, preferred_element_type=F32)
        return d(hi, m) + d(lo, m) + d(hi, ml)
    def forward(x):
        return swap(right(swap(left(x, 0)), 1))
    def inverse(x):
        return swap(right(swap(left(x, 1)), 0))
    def quad(a, b, c, d):
        return jnp.concatenate([jnp.concatenate([a, b], axis=1), jnp.concatenate([c, d], axis=1)], axis=0)
    w = quad(w_ref[0], w_ref[1], w_ref[0], w_ref[1])
    lane = lax.broadcasted_iota(jnp.int32, (1, 512), 1)
    def total(x):
        s = jnp.sum(x, axis=0, keepdims=True)
        a = jnp.sum(s[:, :256], axis=1, keepdims=True)
        b = jnp.sum(s[:, 256:], axis=1, keepdims=True)
        return jnp.where(lane < 256, a, b)
    hits = acc_ref[1024:1280]
    hits = quad(hits, hits, hits, hits)
    field = quad(acc_ref[0:256], acc_ref[256:512], acc_ref[512:768], acc_ref[768:1024])
    residual = w * forward(field)
    direction = residual
    norm = total(residual * residual)
    estimate = None
    for step in range(ITERS):
        image = w * forward(hits * inverse(w * direction)) + DAMPING * direction
        alpha = norm / (total(direction * image) + EPS)
        if step == 0:
            estimate = alpha * direction
        else:
            estimate = estimate + alpha * direction
        if step + 1 < ITERS:
            residual = residual - alpha * image
            new = total(residual * residual)
            direction = residual + (new / (norm + EPS)) * direction
            norm = new
    model = inverse(w * estimate)
    out_ref[0, 0] = model[:256, :256]
    out_ref[0, 1] = model[:256, 256:]
    out_ref[1, 0] = model[256:, :256]
    out_ref[1, 1] = model[256:, 256:]

def on_device(traces, routes, cells, band_bins, spectral_weight):
    n_freq = lax.axis_size("freq")
    rows = traces.shape[0]
    all_bins = lax.all_to_all(jnp.broadcast_to(band_bins[None, :], (n_freq, 2)), "freq", 0, 0, tiled=True).reshape(16)
    vm = pl.BlockSpec(memory_space=pltpu.VMEM)
    params = pltpu.CompilerParams(vmem_limit_bytes=60 * 1024 * 1024)
    msgs = pl.pallas_call(
        prepare_kernel,
        out_shape=jax.ShapeDtypeStruct((32, 32, 128), BF),
        in_specs=[pl.BlockSpec(memory_space=pltpu.SMEM), vm, vm, vm],
        out_specs=vm,
        compiler_params=params,
        name="prepare",
    )(all_bins, traces, routes.reshape(1, rows), cells.reshape(1, rows))
    arrived = lax.all_to_all(msgs, "patch", 0, 0, tiled=True)
    vals, codes = pl.pallas_call(
        regroup_kernel,
        out_shape=[jax.ShapeDtypeStruct((8, 96, 128), BF), jax.ShapeDtypeStruct((48, 128), BF)],
        in_specs=[vm], out_specs=[vm, vm], compiler_params=params,
        name="regroup",
    )(arrived)
    both = jnp.concatenate([vals, jnp.broadcast_to(codes[None], (8, 48, 128))], axis=1)
    both = lax.all_to_all(both, "freq", 0, 0, tiled=True)
    out = pl.pallas_call(
        solve_kernel,
        out_shape=jax.ShapeDtypeStruct((2, 2, 256, 256), F32),
        in_specs=[vm] * 4, out_specs=vm,
        scratch_shapes=[pltpu.VMEM((1280, 256), F32)],
        compiler_params=params,
        name="solve",
    )(both[:, :96], both[:, 96:], spectral_weight.reshape(2, 256, 256), jnp.asarray(kernel_table()))
    return out.reshape(2, 2, 65536)


def solution(mesh):
    return jax.shard_map(
        on_device,
        mesh=mesh,
        in_specs=(P(("patch", "freq"), None), P(("patch", "freq"), None), P(("patch", "freq")), P("freq"), P("freq", "patch")),
        out_specs=P(None, "freq", "patch"),
        check_vma=False,
    )
```

```python
import functools, math
import jax
import jax.numpy as jnp
import numpy as np
from jax import lax
from jax.experimental import pallas as pl
from jax.experimental.pallas import tpu as pltpu
F32=jnp.float32; BF=jnp.bfloat16
NTD=(((1,),(1,)),((),()))


def cosine(phase, n):
    quad = (phase + n // 8) // (n // 4)
    rest = (phase - quad * (n // 4)).astype(F32) * (2.0 * math.pi / n)
    sq = rest * rest
    c = 1.0 + sq * (-0.5 + sq * (1.0/24 + sq * (-1.0/720 + sq * (1.0/40320))))
    s = rest * (1.0 + sq * (-1.0/6 + sq * (1.0/120 + sq * (-1.0/5040))))
    odd = (quad & 1) == 1
    val = jnp.where(odd, s, c)
    neg = ((quad + 1) & 2) == 2
    return jnp.where(neg, -val, val)

def make_basis(bins_ref, nt):
    sub = lax.broadcasted_iota(jnp.int32, (8, 128), 0)
    k = jnp.concatenate([jnp.where(sub < 4, bins_ref[2 * i], bins_ref[2 * i + 1]) for i in range(4)], axis=0)
    part = (lax.broadcasted_iota(jnp.int32, (32, 128), 0) // 2) & 1
    t = lax.broadcasted_iota(jnp.int32, (32, nt), 1)
    kk = jnp.concatenate([k] * (nt // 128), axis=1)
    pp = jnp.concatenate([part * (nt // 4)] * (nt // 128), axis=1)
    phase = (kk * t + pp) & (nt - 1)
    return (cosine(phase, nt) * (1.0 / math.sqrt(nt))).astype(BF)

def routing(route, cell):
    rows = route.shape[1]
    member = (lax.broadcasted_iota(jnp.int32, (32, rows), 0) == route).astype(F32)
    tri = (lax.broadcasted_iota(jnp.int32, (128, 128), 0) < lax.broadcasted_iota(jnp.int32, (128, 128), 1)).astype(F32).astype(BF)
    pieces = [member[:, 128*i:128*i+128] for i in range(rows // 128)]
    inside = jnp.dot(jnp.concatenate(pieces, axis=0).astype(BF), tri, preferred_element_type=F32)
    offset = jnp.zeros((32, 1), F32)
    before = []
    for i, piece in enumerate(pieces):
        before.append(inside[32*i:32*i+32] + offset)
        offset = offset + jnp.sum(piece, axis=1, keepdims=True)
    rank = jnp.sum(member * jnp.concatenate(before, axis=1), axis=0, keepdims=True).astype(jnp.int32)
    return route * 32 + (rank & 31), rank >> 5

def stack_rows(spectra, third, cell):
    rows = spectra.shape[1]
    out = [jnp.where(third == q, spectra, 0.0) for q in range(3)]
    r = lax.broadcasted_iota(jnp.int32, (32, rows), 0)
    high = ((cell >> 8) + 1).astype(F32)
    low = (cell & 255).astype(F32)
    code = jnp.where((r & 4) == 0, high, low)
    out.append(jnp.where((r >> 3) == third, code, 0.0))
    return jnp.concatenate(out, axis=0).astype(BF)

def one_hot_rows(key):
    rows = key.shape[1]
    return jnp.where(lax.broadcasted_iota(jnp.int32, (1024, rows), 0) == key, 1.0, 0.0).astype(BF)

def write_messages(packed, msg_ref):
    lane = lax.broadcasted_iota(jnp.int32, (32, 128), 1) >> 5
    for cb in range(8):
        groups = [packed[32*g:32*g+32, 128*cb:128*cb+128] for g in range(4)]
        for pm in range(4):
            out = jnp.zeros((32, 128), F32)
            for g in range(4):
                piece = groups[g]
                shift = (32 * (g - pm)) % 128
                if shift:
                    piece = pltpu.roll(piece, shift, 1)
                out = jnp.where(lane == g, piece, out)
            msg_ref[4*cb+pm] = out.astype(BF)

def regroup(msg_ref, pair_ref):
    lane = lax.broadcasted_iota(jnp.int32, (32, 128), 1) >> 5
    lane8 = lane[:8]
    sub = lax.broadcasted_iota(jnp.int32, (8, 128), 0)
    dense, codes = [], []
    for h in range(8):
        msgs = [msg_ref[4*h+i].astype(F32) for i in range(4)]
        for k in range(3):
            last = pltpu.roll(msgs[3], 96 - 32*k, 1)
            dense.append(jnp.where(lane < 3, msgs[k], last))
            out = msgs[3][8*k:8*k+8]
            for q in range(3):
                out = jnp.where(lane8 == q, pltpu.roll(msgs[k][8*q:8*q+8], 32 + 32*q, 1), out)
            codes.append(out)
    for f in range(8):
        tiles = []
        for pair in range(12):
            a = dense[2*pair][8*(f//2):8*(f//2)+8]
            b = dense[2*pair+1][8*(f//2):8*(f//2)+8]
            if f % 2 == 0:
                b = pltpu.roll(b, 4, 0)
            else:
                a = pltpu.roll(a, 4, 0)
            tiles.append(jnp.where(sub < 4, a, b))
        pair_ref[f, 0:96, :] = jnp.concatenate(tiles, axis=0).astype(BF)
    out = []
    for cg in range(6):
        t = codes[4*cg]
        for i in range(1, 4):
            t = jnp.where((sub & 3) == i, codes[4*cg+i], t)
        out.append(t)
    out = jnp.concatenate(out, axis=0).astype(BF)
    for f in range(8):
        pair_ref[f, 96:144, :] = out
from jax.sharding import PartitionSpec as P
SIDE=16; ITERS=2; EPS=1e-6; DAMPING=0.1

def kernel_table():
    flat = np.arange(256)
    up, lo = flat // SIDE, flat % SIDE
    phase = (up[:, None] * up[None, :] + lo[:, None] * lo[None, :]) % SIDE
    angle = 2.0 * np.pi / SIDE * phase
    return np.stack([np.cos(angle) / SIDE, -np.sin(angle) / SIDE]).astype(np.float32)

def bin_step(vals, codes, cg, iota, comps=4):
    u = jnp.concatenate([codes[8*cg+i:8*cg+i+1] for i in range(4)], axis=1)
    l = jnp.concatenate([codes[8*cg+4+i:8*cg+5+i] for i in range(4)], axis=1)
    mask = (iota + 1.0) == u
    rhs = jnp.where(iota == l, 1.0, 0.0).astype(BF)
    rows = []
    for c in range(comps):
        v = jnp.concatenate([vals[4*(4*cg+i)+c:4*(4*cg+i)+c+1] for i in range(4)], axis=1)
        rows.append(jnp.where(mask, v, 0.0).astype(BF))
    rows.append(jnp.where(mask, 1.0, 0.0).astype(BF))
    return jnp.concatenate(rows, axis=0), rhs

def split(x):
    hi = x.astype(BF)
    return hi, (x - hi.astype(F32)).astype(BF)

def swap(x):
    return jnp.concatenate([jnp.concatenate([x[:256,:256], x[256:,:256]], axis=1),
                            jnp.concatenate([x[:256,256:], x[256:,256:]], axis=1)], axis=0)

def solve_kernel(pair_ref, w_ref, tab_ref, out_ref, acc_ref):
    acc_ref[...] = jnp.zeros_like(acc_ref)
    @pl.loop(0, 8)
    def _(g):
        vals = pair_ref[g, 0:96, :].astype(F32)
        codes = pair_ref[g, 96:144, :].astype(F32)
        iota = lax.broadcasted_iota(jnp.int32, (256, 512), 0).astype(F32)
        for cg in range(6):
            lhs, rhs = bin_step(vals, codes, cg, iota)
            acc_ref[...] += lax.dot_general(lhs, rhs, NTD, preferred_element_type=F32)
    kr, krl = split(tab_ref[0])
    ki, kil = split(tab_ref[1])

    def quad(a, b, c, d):
        return jnp.concatenate([jnp.concatenate([a, b], axis=1), jnp.concatenate([c, d], axis=1)], axis=0)

    tables = (quad(kr, -ki, ki, kr), quad(krl, -kil, kil, krl), quad(kr, ki, -ki, kr), quad(krl, kil, -kil, krl))
    dot = functools.partial(jnp.dot, preferred_element_type=F32)

    def left(x, which):
        hi, lo = split(x)
        m, ml = tables[2 * which], tables[2 * which + 1]
        return dot(m, hi) + dot(m, lo) + dot(ml, hi)

    def right(x, which):
        hi, lo = split(x)
        m, ml = tables[2 * which], tables[2 * which + 1]
        return dot(hi, m) + dot(lo, m) + dot(hi, ml)

    def forward(x):
        return swap(right(swap(left(x, 0)), 1))
    def inverse(x):
        return swap(right(swap(left(x, 1)), 0))
    def plane(f):
        return jnp.concatenate([w_ref[pl.ds(2 * h + f, 256, stride=4), :] for h in range(2)], axis=1)

    w0, w1 = plane(0), plane(1)
    w = quad(w0, w1, w0, w1)
    lane = lax.broadcasted_iota(jnp.int32, (1, 512), 1)
    def total(x):
        s = jnp.sum(x, axis=0, keepdims=True)
        a = jnp.sum(s[:, :256], axis=1, keepdims=True)
        b = jnp.sum(s[:, 256:], axis=1, keepdims=True)
        return jnp.where(lane < 256, a, b)
    hits = acc_ref[1024:1280]
    hits = quad(hits, hits, hits, hits)
    field = quad(acc_ref[0:256], acc_ref[256:512], acc_ref[512:768], acc_ref[768:1024])
    residual = w * forward(field)
    direction = residual
    norm = total(residual * residual)
    estimate = None
    for step in range(ITERS):
        image = w * forward(hits * inverse(w * direction)) + DAMPING * direction
        alpha = norm / (total(direction * image) + EPS)
        if step == 0:
            estimate = alpha * direction
        else:
            estimate = estimate + alpha * direction
        if step + 1 < ITERS:
            residual = residual - alpha * image
            new = total(residual * residual)
            direction = residual + (new / (norm + EPS)) * direction
            norm = new
    model = inverse(w * estimate)
    for part in range(2):
        for f in range(2):
            for h in range(2):
                out_ref[part, pl.ds(2 * h + f, 256, stride=4), :] = model[256 * part:256 * part + 256, 256 * f + 128 * h:256 * f + 128 * h + 128]


def peer_loop(n, me, body):
    lax.fori_loop(1, n, lambda i, carry: (body(lax.rem(me + i, n)), carry)[1], 0)


def exchange_kernel(bins_ref, traces_ref, route_ref, cell_ref, out_ref,
                    traces_vm, hot_vm, bins_vm, msg_out, msg_in, pair_out,
                    trace_sem, bin_send, bin_recv, msg_send, msg_recv, pair_send, pair_recv):
    me_p, me_f = lax.axis_index("patch"), lax.axis_index("freq")
    barrier = pltpu.get_barrier_semaphore()
    mesh_id = pl.DeviceIdType.MESH
    peer_loop(8, me_f, lambda f: pl.semaphore_signal(barrier, inc=1, device_id={"freq": f}, device_id_type=mesh_id))
    peer_loop(32, me_p, lambda p: pl.semaphore_signal(barrier, inc=1, device_id={"patch": p}, device_id_type=mesh_id))
    fetch = pltpu.make_async_copy(traces_ref, traces_vm, trace_sem)
    fetch.start()
    sub = lax.broadcasted_iota(jnp.int32, (8, 128), 0)
    bins_vm[me_f] = jnp.where((sub & 1) == 1, bins_ref[1], bins_ref[0])
    key, third = routing(route_ref[...], cell_ref[...])
    hot_vm[...] = one_hot_rows(key)
    pl.semaphore_wait(barrier, 38)

    def bin_copy(f, slot):
        return pltpu.make_async_remote_copy(
            src_ref=bins_vm.at[me_f], dst_ref=bins_vm.at[slot], send_sem=bin_send.at[f],
            recv_sem=bin_recv.at[slot], device_id={"freq": f}, device_id_type=mesh_id)

    def msg_copy(p, slot):
        return pltpu.make_async_remote_copy(
            src_ref=msg_out.at[p], dst_ref=msg_in.at[slot], send_sem=msg_send.at[p],
            recv_sem=msg_recv.at[slot], device_id={"patch": p}, device_id_type=mesh_id)

    def pair_copy(f, slot):
        return pltpu.make_async_remote_copy(
            src_ref=pair_out.at[f], dst_ref=out_ref.at[slot], send_sem=pair_send.at[f],
            recv_sem=pair_recv.at[slot], device_id={"freq": f}, device_id_type=mesh_id)

    peer_loop(8, me_f, lambda f: bin_copy(f, me_f).start())
    peer_loop(8, me_f, lambda f: bin_copy(f, f).wait_recv())
    basis = make_basis(bins_vm, traces_vm.shape[1])
    fetch.wait()
    spectra = lax.dot_general(basis, traces_vm[...], NTD, preferred_element_type=F32)
    stacked = stack_rows(spectra, third, cell_ref[...])
    packed = lax.dot_general(stacked, hot_vm[...], NTD, preferred_element_type=F32)
    write_messages(packed, msg_out)
    peer_loop(32, me_p, lambda p: msg_copy(p, me_p).start())
    msg_in[me_p] = msg_out[me_p]
    peer_loop(32, me_p, lambda p: msg_copy(p, p).wait_recv())
    regroup(msg_in, pair_out)
    peer_loop(8, me_f, lambda f: pair_copy(f, me_f).start())
    own = pltpu.make_async_copy(pair_out.at[me_f], out_ref.at[me_f], trace_sem)
    own.start()
    peer_loop(8, me_f, lambda f: bin_copy(f, me_f).wait_send())
    peer_loop(32, me_p, lambda p: msg_copy(p, me_p).wait_send())
    own.wait()
    peer_loop(8, me_f, lambda f: pair_copy(f, f).wait_recv())
    peer_loop(8, me_f, lambda f: pair_copy(f, me_f).wait_send())

def on_device(traces, routes, cells, band_bins, spectral_weight):
    rows = traces.shape[0]
    vm = pl.BlockSpec(memory_space=pltpu.VMEM)
    sm = pl.BlockSpec(memory_space=pltpu.SMEM)
    anywhere = pl.BlockSpec(memory_space=pl.ANY)
    dma = pltpu.SemaphoreType.DMA
    both = pl.pallas_call(
        exchange_kernel,
        out_shape=jax.ShapeDtypeStruct((8, 144, 128), BF),
        in_specs=[sm, anywhere, vm, vm],
        out_specs=anywhere,
        scratch_shapes=[
            pltpu.VMEM(traces.shape, BF), pltpu.VMEM((1024, rows), BF), pltpu.VMEM((8, 8, 128), jnp.int32),
            pltpu.VMEM((32, 32, 128), BF), pltpu.VMEM((32, 32, 128), BF), pltpu.VMEM((8, 144, 128), BF),
            dma, dma((8,)), dma((8,)), dma((32,)), dma((32,)), dma((8,)), dma((8,)),
        ],
        compiler_params=pltpu.CompilerParams(
            collective_id=0, has_side_effects=True, vmem_limit_bytes=48 * 1024 * 1024),
        name="exchange",
    )(band_bins, traces, routes.reshape(1, rows), cells.reshape(1, rows))
    weight = spectral_weight.reshape(2, 512, 128).transpose(1, 0, 2).reshape(1024, 128)
    out = pl.pallas_call(
        solve_kernel,
        out_shape=jax.ShapeDtypeStruct((2, 1024, 128), F32),
        in_specs=[vm] * 3, out_specs=vm,
        scratch_shapes=[pltpu.VMEM((1280, 256), F32)],
        compiler_params=pltpu.CompilerParams(vmem_limit_bytes=60 * 1024 * 1024),
        name="solve",
    )(both, weight, jnp.asarray(kernel_table()))
    return out.reshape(2, 512, 2, 128).transpose(0, 2, 1, 3).reshape(2, 2, 65536)


def solution(mesh):
    return jax.shard_map(
        on_device,
        mesh=mesh,
        in_specs=(P(("patch", "freq"), None), P(("patch", "freq"), None), P(("patch", "freq")), P("freq"), P("freq", "patch")),
        out_specs=P(None, "freq", "patch"),
        check_vma=False,
    )
```

```python
import functools, math
import jax
import jax.numpy as jnp
import ml_dtypes
import numpy as np
from jax import lax
from jax.experimental import pallas as pl
from jax.experimental.pallas import tpu as pltpu
F32=jnp.float32; BF=jnp.bfloat16
NTD=(((1,),(1,)),((),()))


def cosine(phase, n):
    quad = (phase + n // 8) // (n // 4)
    rest = (phase - quad * (n // 4)).astype(F32) * (2.0 * math.pi / n)
    sq = rest * rest
    c = 1.0 + sq * (-0.5 + sq * (1.0/24 + sq * (-1.0/720 + sq * (1.0/40320))))
    s = rest * (1.0 + sq * (-1.0/6 + sq * (1.0/120 + sq * (-1.0/5040))))
    odd = (quad & 1) == 1
    val = jnp.where(odd, s, c)
    neg = ((quad + 1) & 2) == 2
    return jnp.where(neg, -val, val)

def make_basis(bins_ref, nt):
    sub = lax.broadcasted_iota(jnp.int32, (8, 128), 0)
    k = jnp.concatenate([jnp.where(sub < 4, bins_ref[2 * i], bins_ref[2 * i + 1]) for i in range(4)], axis=0)
    part = (lax.broadcasted_iota(jnp.int32, (32, 128), 0) // 2) & 1
    t = lax.broadcasted_iota(jnp.int32, (32, nt), 1)
    kk = jnp.concatenate([k] * (nt // 128), axis=1)
    pp = jnp.concatenate([part * (nt // 4)] * (nt // 128), axis=1)
    phase = (kk * t + pp) & (nt - 1)
    return (cosine(phase, nt) * (1.0 / math.sqrt(nt))).astype(BF)

def routing(route, cell):
    rows = route.shape[1]
    key = (route << 26) + (cell << 10) + lax.broadcasted_iota(jnp.int32, (1, rows), 1)
    smaller = jnp.zeros((8, rows), F32)
    for a in range(rows // 128):
        column = jnp.broadcast_to(key[:, 128 * a:128 * a + 128], (128, 128)).T
        for i in range(16):
            part = jnp.concatenate([column[8 * i:8 * i + 8]] * (rows // 128), axis=1)
            smaller = smaller + jnp.where(part < key, 1.0, 0.0)
    patch = lax.broadcasted_iota(jnp.int32, (32, rows), 0)
    before = jnp.sum(jnp.where(route < patch, 1.0, 0.0), axis=1, keepdims=True)
    rank = jnp.sum(smaller, axis=0, keepdims=True) - jnp.sum(jnp.where(route == patch, before, 0.0), axis=0, keepdims=True)
    rank = rank.astype(jnp.int32)
    return route * 32 + (rank & 31), rank >> 5

def stack_rows(spectra, third, cell):
    rows = spectra.shape[1]
    out = [jnp.where(third == q, spectra, 0.0) for q in range(3)]
    r = lax.broadcasted_iota(jnp.int32, (32, rows), 0)
    high = ((cell >> 8) + 1).astype(F32)
    low = (cell & 255).astype(F32)
    code = jnp.where((r & 4) == 0, high, low)
    out.append(jnp.where((r >> 3) == third, code, 0.0))
    return jnp.concatenate(out, axis=0).astype(BF)

def one_hot_rows(key):
    rows = key.shape[1]
    return jnp.where(lax.broadcasted_iota(jnp.int32, (1024, rows), 0) == key, 1.0, 0.0).astype(BF)

def write_messages(packed, turn, msg_ref):
    lane = lax.broadcasted_iota(jnp.int32, (32, 128), 1) >> 5
    for cb in range(8):
        groups = [packed[32*g:32*g+32, 128*cb:128*cb+128] for g in range(4)]
        for pm in range(4):
            out = jnp.zeros((32, 128), F32)
            for g in range(4):
                piece = groups[g]
                shift = (32 * (g - pm)) % 128
                if shift:
                    piece = pltpu.roll(piece, shift, 1)
                out = jnp.where(lane == g, piece, out)
            msg_ref[4*cb+pm] = pltpu.roll(out, turn, 1).astype(BF)

def regroup(msg_ref, sources, pair_ref):
    lane = lax.broadcasted_iota(jnp.int32, (32, 128), 1) >> 3
    lane8 = lane[:8]
    sub = lax.broadcasted_iota(jnp.int32, (8, 128), 0)
    msgs = [msg_ref[sources[t]].astype(F32) for t in range(16)]
    dense, codes = [], []
    for b in range(12):
        q = b // 4
        value, code = msgs[0], msgs[0][8 * q:8 * q + 8]
        for t in range(1, 16):
            value = jnp.where(lane == (b + t) % 16, msgs[t], value)
            code = jnp.where(lane8 == (12 + b % 4 + t) % 16, msgs[t][8 * q:8 * q + 8], code)
        dense.append(value)
        codes.append(pltpu.roll(code, 32 + 32 * q, 1))
    for f in range(8):
        tiles = []
        for pair in range(6):
            a = dense[2 * pair][8 * (f // 2):8 * (f // 2) + 8]
            b = dense[2 * pair + 1][8 * (f // 2):8 * (f // 2) + 8]
            if f % 2 == 0:
                b = pltpu.roll(b, 4, 0)
            else:
                a = pltpu.roll(a, 4, 0)
            tiles.append(jnp.where(sub < 4, a, b))
        pair_ref[f, 0:48, :] = jnp.concatenate(tiles, axis=0).astype(BF)
    out = []
    for cg in range(3):
        t = codes[4 * cg]
        for i in range(1, 4):
            t = jnp.where((sub & 3) == i, codes[4 * cg + i], t)
        out.append(t)
    out = jnp.concatenate(out, axis=0).astype(BF)
    for f in range(8):
        pair_ref[f, 48:72, :] = out
from jax.sharding import PartitionSpec as P
SIDE = 16
EPS = 1e-6
DAMPING = 0.1
STRETCH = 1.135235
CENTER = 0.99785729


def kernel_table():
    flat = np.arange(256)
    up, lo = flat // SIDE, flat % SIDE
    phase = (up[:, None] * up[None, :] + lo[:, None] * lo[None, :]) % SIDE
    angle = 2.0 * np.pi / SIDE * phase
    table = np.stack([np.cos(angle), -np.sin(angle)]) * STRETCH
    return table.astype(ml_dtypes.bfloat16).astype(np.float32)


TABLE_SCALE = 1.0 / (STRETCH * CENTER * SIDE) ** 2


WINDOW = 112


def bin_step(values, u, l, low, acc_ref):
    n = u.shape[1]
    iota_u = lax.broadcasted_iota(jnp.int32, (WINDOW, n), 0).astype(F32).astype(BF)
    iota_l = lax.broadcasted_iota(jnp.int32, (256, n), 0).astype(F32).astype(BF)
    one, zero = jnp.ones((), BF), jnp.zeros((), BF)
    start = pl.multiple_of(jnp.minimum(low, 256 - WINDOW), 8)
    mask = iota_u == jnp.where(u >= low.astype(F32), u - start.astype(F32), -1.0).astype(BF)
    parts = [jnp.where(mask, values[c:c + 1].astype(BF), zero) for c in range(4)] + [jnp.where(mask, one, zero)]
    hot = jnp.where(iota_l == l.astype(BF), one, zero)
    sums = lax.dot_general(jnp.concatenate(parts, axis=0), hot, NTD, preferred_element_type=F32)
    for c in range(5):
        acc_ref[c, pl.ds(start, WINDOW), :] += sums[WINDOW * c:WINDOW * c + WINDOW]


def spread(pair_ref, val_ref, code_ref):
    lane = lax.broadcasted_iota(jnp.int32, (8, 128), 1)
    first, last = jnp.zeros((8, 128), F32), jnp.zeros((8, 128), F32)
    lows, highs = [None] * 3, [None] * 3
    for half in range(2):
        for g in range(8):
            at = 128 * (8 * half + g)
            vals = pair_ref[half, g, 0:48, :].astype(F32)
            codes = pair_ref[half, g, 48:72, :].astype(F32)
            for cg in range(3):
                code = codes[8 * cg:8 * cg + 8]
                val_ref[cg, :, at:at + 128] = vals[16 * cg:16 * cg + 16]
                code_ref[cg, :, at:at + 128] = code
                low = jnp.where(code < 1.0, 999.0, code)
                lows[cg] = low if lows[cg] is None else jnp.minimum(lows[cg], low)
                highs[cg] = code if highs[cg] is None else jnp.maximum(highs[cg], code)
    for cg in range(3):
        first = jnp.where(lane == cg, jnp.min(lows[cg], axis=1, keepdims=True) - 1.0, first)
        last = jnp.where(lane == cg, jnp.max(highs[cg], axis=1, keepdims=True) - 1.0, last)
    return first.astype(jnp.int32), last.astype(jnp.int32)


def split(x):
    hi = x.astype(BF)
    return hi, (x - hi.astype(F32)).astype(BF)


def quad(a, b, c, d):
    return jnp.concatenate([jnp.concatenate([a, b], axis=1), jnp.concatenate([c, d], axis=1)], axis=0)


def swap(x):
    return quad(x[:256, :256], x[256:, :256], x[:256, 256:], x[256:, 256:])


def fit(acc_ref, w_ref, tab_ref, out_ref):
    kr, ki = tab_ref[0].astype(BF), tab_ref[1].astype(BF)
    plain, conj = quad(kr, -ki, ki, kr), quad(kr, ki, -ki, kr)
    dot = functools.partial(jnp.dot, preferred_element_type=F32)

    def left(x, m):
        return dot(jnp.concatenate([m, m], axis=1), jnp.concatenate(split(x), axis=0))

    def right(x, m):
        return dot(jnp.concatenate(split(x), axis=1), jnp.concatenate([m, m], axis=0))

    def forward(x):
        return swap(right(swap(left(x, plain)), conj))

    def inverse(x):
        return swap(right(swap(left(x, conj)), plain))

    def plane(f):
        return jnp.concatenate([w_ref[pl.ds(2 * h + f, 256, stride=4), :] for h in range(2)], axis=1)

    w0, w1 = plane(0) * TABLE_SCALE, plane(1) * TABLE_SCALE
    w = quad(w0, w1, w0, w1)
    lane = lax.broadcasted_iota(jnp.int32, (1, 512), 1)

    def total(x):
        s = jnp.sum(x, axis=0, keepdims=True)
        a = jnp.sum(s[:, :256], axis=1, keepdims=True)
        b = jnp.sum(s[:, 256:], axis=1, keepdims=True)
        return jnp.where(lane < 256, a, b)

    hits = acc_ref[4]
    hits = quad(hits, hits, hits, hits)
    field = quad(acc_ref[0], acc_ref[1], acc_ref[2], acc_ref[3])
    residual = w * forward(field)
    norm = total(residual * residual)
    g0 = inverse(w * residual)
    pulled = hits * g0
    alpha = norm / (total(pulled * g0) + DAMPING * norm + EPS)
    direction = residual
    residual = residual - alpha * (w * forward(pulled) + DAMPING * direction)
    new = total(residual * residual)
    direction = residual + (new / (norm + EPS)) * direction
    g1 = inverse(w * direction)
    beta = new / (total(hits * g1 * g1) + DAMPING * total(direction * direction) + EPS)
    model = alpha * g0 + beta * g1
    for part in range(2):
        for f in range(2):
            for h in range(2):
                out_ref[part, pl.ds(2 * h + f, 256, stride=4), :] = model[
                    256 * part:256 * part + 256, 256 * f + 128 * h:256 * f + 128 * h + 128]


def solve_kernel(pair_ref, w_hbm, tab_hbm, out_ref, acc_ref, w_ref, tab_ref, val_ref, code_ref, span_vm, span_sm, sems):
    fetch = [pltpu.make_async_copy(w_hbm, w_ref, sems.at[0]), pltpu.make_async_copy(tab_hbm, tab_ref, sems.at[1])]
    for copy in fetch:
        copy.start()
    span_vm[0], span_vm[1] = spread(pair_ref, val_ref, code_ref)
    spans = pltpu.make_async_copy(span_vm, span_sm, sems.at[2])
    spans.start()
    acc_ref[...] = jnp.zeros_like(acc_ref)
    spans.wait()

    @pl.loop(0, 3)
    def _(cg):
        for i in range(4):
            first, last = span_sm[0, i, cg], span_sm[1, i, cg]
            first = (first // 8) * 8
            wide = last - first
            count = sum((wide >= WINDOW * k).astype(jnp.int32) for k in range(-(-256 // WINDOW)))

            @pl.loop(0, count)
            def _(again):
                code = code_ref[cg]
                bin_step(val_ref[cg, 4 * i:4 * i + 4, :], code[i:i + 1] - 1.0, code[4 + i:5 + i], first + again * WINDOW, acc_ref)

    for copy in fetch:
        copy.wait()
    fit(acc_ref, w_ref, tab_ref, out_ref)


MESH_ID = pl.DeviceIdType.MESH


def peer_loop(n, me, body):
    lax.fori_loop(1, n, lambda i, carry: (body(lax.rem(me + i, n)), carry)[1], 0)


def exchange_kernel(bins_ref, traces_ref, route_ref, cell_ref, out_ref,
                    traces_vm, hot_vm, bins_vm, msg_out, msg_in, pair_out,
                    trace_sem, own_sem, bin_send, bin_recv, msg_send, msg_recv, pair_send, pair_recv):
    me_p, me_f = lax.axis_index("patch"), lax.axis_index("freq")
    me_x, me_z = me_p // 8, lax.rem(me_p, 8)
    barrier = pltpu.get_barrier_semaphore()
    peer_loop(8, me_f, lambda f: pl.semaphore_signal(barrier, inc=1, device_id={"freq": f}, device_id_type=MESH_ID))
    peer_loop(32, me_p, lambda p: pl.semaphore_signal(barrier, inc=1, device_id={"patch": p}, device_id_type=MESH_ID))
    fetch = pltpu.make_async_copy(traces_ref, traces_vm, trace_sem)
    fetch.start()
    sub = lax.broadcasted_iota(jnp.int32, (8, 128), 0)
    bins_vm[me_f] = jnp.where((sub & 1) == 1, bins_ref[1], bins_ref[0])
    key, third = routing(route_ref[...], cell_ref[...])
    hot_vm[...] = one_hot_rows(key)

    def bin_copy(f, slot):
        return pltpu.make_async_remote_copy(
            src_ref=bins_vm.at[me_f], dst_ref=bins_vm.at[slot], send_sem=bin_send.at[f],
            recv_sem=bin_recv.at[slot], device_id={"freq": f}, device_id_type=MESH_ID)

    def msg_copy(p, slot):
        return pltpu.make_async_remote_copy(
            src_ref=msg_out.at[p], dst_ref=msg_in.at[slot], send_sem=msg_send.at[p],
            recv_sem=msg_recv.at[slot], device_id={"patch": p}, device_id_type=MESH_ID)

    def pair_copy(half, f, slot):
        return pltpu.make_async_remote_copy(
            src_ref=pair_out.at[half, f], dst_ref=out_ref.at[half, slot], send_sem=pair_send.at[half, f],
            recv_sem=pair_recv.at[half, slot], device_id={"freq": f}, device_id_type=MESH_ID)

    def own_copy(half):
        return pltpu.make_async_copy(pair_out.at[half, me_f], out_ref.at[half, me_f], own_sem.at[half])

    pl.semaphore_wait(barrier, 38)
    peer_loop(8, me_f, lambda f: bin_copy(f, me_f).start())
    peer_loop(8, me_f, lambda f: bin_copy(f, f).wait_recv())
    basis = make_basis(bins_vm, traces_vm.shape[1])
    fetch.wait()
    spectra = lax.dot_general(basis, traces_vm[...], NTD, preferred_element_type=F32)
    stacked = stack_rows(spectra, third, cell_ref[...])
    packed = lax.dot_general(stacked, hot_vm[...], NTD, preferred_element_type=F32)
    write_messages(packed, 8 * lax.rem(me_p, 16), msg_out)
    order = [(i // 8, i % 8) for i in range(32)]
    targets = [lax.rem(me_x + dx, 4) * 8 + lax.rem(me_z + dz, 8) for dx, dz in order]
    sources = [lax.rem(me_x + 4 - dx, 4) * 8 + lax.rem(me_z + 8 - dz, 8) for dx, dz in order]
    for p in targets[1:]:
        msg_copy(p, me_p).start()
    msg_in[me_p] = msg_out[me_p]
    for half in range(2):
        for p in sources[max(1, 16 * half):16 * half + 16]:
            msg_copy(p, p).wait_recv()
        first = lax.rem(me_x + 2 * half, 4)
        second = lax.rem(me_x + 2 * half + 3, 4)
        is_odd = lax.rem(me_x, 2)
        planes = (first + is_odd * (second - first), second + is_odd * (first - second))
        regroup(msg_in, [planes[t // 8] * 8 + t % 8 for t in range(16)], pair_out.at[half])
        peer_loop(8, me_f, lambda f: pair_copy(half, f, me_f).start())
        own_copy(half).start()
    peer_loop(8, me_f, lambda f: bin_copy(f, me_f).wait_send())
    for p in targets[1:]:
        msg_copy(p, me_p).wait_send()
    for half in range(2):
        own_copy(half).wait()
        peer_loop(8, me_f, lambda f: pair_copy(half, f, f).wait_recv())
        peer_loop(8, me_f, lambda f: pair_copy(half, f, me_f).wait_send())

def on_device(traces, routes, cells, band_bins, spectral_weight):
    rows = traces.shape[0]
    vm = pl.BlockSpec(memory_space=pltpu.VMEM)
    sm = pl.BlockSpec(memory_space=pltpu.SMEM)
    anywhere = pl.BlockSpec(memory_space=pl.ANY)
    dma = pltpu.SemaphoreType.DMA
    both = pl.pallas_call(
        exchange_kernel,
        out_shape=jax.ShapeDtypeStruct((2, 8, 72, 128), BF),
        in_specs=[sm, anywhere, vm, vm],
        out_specs=anywhere,
        scratch_shapes=[
            pltpu.VMEM(traces.shape, BF), pltpu.VMEM((1024, rows), BF), pltpu.VMEM((8, 8, 128), jnp.int32),
            pltpu.VMEM((32, 32, 128), BF), pltpu.VMEM((32, 32, 128), BF), pltpu.VMEM((2, 8, 72, 128), BF),
            dma, dma((2,)), dma((8,)), dma((8,)), dma((32,)), dma((32,)), dma((2, 8)), dma((2, 8)),
        ],
        compiler_params=pltpu.CompilerParams(
            collective_id=0, has_side_effects=True, vmem_limit_bytes=62 * 1024 * 1024),
        name="exchange",
    )(band_bins, traces, routes.reshape(1, rows), cells.reshape(1, rows))
    weight = spectral_weight.reshape(2, 512, 128).transpose(1, 0, 2).reshape(1024, 128)
    out = pl.pallas_call(
        solve_kernel,
        out_shape=jax.ShapeDtypeStruct((2, 1024, 128), F32),
        in_specs=[vm, anywhere, anywhere], out_specs=vm,
        scratch_shapes=[
            pltpu.VMEM((5, 256, 256), F32), pltpu.VMEM((1024, 128), F32), pltpu.VMEM((2, 256, 256), F32),
            pltpu.VMEM((3, 16, 2048), F32), pltpu.VMEM((3, 8, 2048), F32),
            pltpu.VMEM((2, 8, 128), jnp.int32), pltpu.SMEM((2, 8, 128), jnp.int32), dma((3,)),
        ],
        compiler_params=pltpu.CompilerParams(vmem_limit_bytes=60 * 1024 * 1024),
        name="solve",
    )(both, weight, jnp.asarray(kernel_table()))
    return out.reshape(2, 512, 2, 128).transpose(0, 2, 1, 3).reshape(2, 2, 65536)


def solution(mesh):
    return jax.shard_map(
        on_device,
        mesh=mesh,
        in_specs=(P(("patch", "freq"), None), P(("patch", "freq"), None), P(("patch", "freq")), P("freq"), P("freq", "patch")),
        out_specs=P(None, "freq", "patch"),
        check_vma=False,
    )
```

```python
import functools, math
import jax
import jax.numpy as jnp
import ml_dtypes
import numpy as np
from jax import lax
from jax.experimental import pallas as pl
from jax.experimental.pallas import tpu as pltpu
F32 = jnp.float32
BF = jnp.bfloat16
CAP = 96
NTD=(((1,),(1,)),((),()))


def cosine(phase, n):
    quad = (phase + n // 8) // (n // 4)
    rest = (phase - quad * (n // 4)).astype(F32) * (2.0 * math.pi / n)
    sq = rest * rest
    c = 1.0 + sq * (-0.5 + sq * (1.0/24 + sq * (-1.0/720 + sq * (1.0/40320))))
    s = rest * (1.0 + sq * (-1.0/6 + sq * (1.0/120 + sq * (-1.0/5040))))
    odd = (quad & 1) == 1
    val = jnp.where(odd, s, c)
    neg = ((quad + 1) & 2) == 2
    return jnp.where(neg, -val, val)

def make_basis(bins_ref, nt):
    sub = lax.broadcasted_iota(jnp.int32, (8, 128), 0)
    k = jnp.concatenate([jnp.where(sub < 4, bins_ref[2 * i], bins_ref[2 * i + 1]) for i in range(4)], axis=0)
    part = (lax.broadcasted_iota(jnp.int32, (32, 128), 0) // 2) & 1
    t = lax.broadcasted_iota(jnp.int32, (32, nt), 1)
    kk = jnp.concatenate([k] * (nt // 128), axis=1)
    pp = jnp.concatenate([part * (nt // 4)] * (nt // 128), axis=1)
    phase = (kk * t + pp) & (nt - 1)
    return (cosine(phase, nt) * (1.0 / math.sqrt(nt))).astype(BF)

def columns_of(row):
    return [jnp.broadcast_to(row[:, a:a + 128], (128, 128)).T for a in range(0, row.shape[1], 128)]


def routing(route, cell):
    rows = route.shape[1]
    key = (route << 26) + (cell << 10) + lax.broadcasted_iota(jnp.int32, (1, rows), 1)
    key_columns = columns_of(key)
    smaller = jnp.zeros((8, rows), F32)
    for column in key_columns:
        for i in range(16):
            part = jnp.concatenate([column[8 * i:8 * i + 8]] * (rows // 128), axis=1)
            smaller = smaller + jnp.where(part < key, 1.0, 0.0)
    patch = lax.broadcasted_iota(jnp.int32, (32, rows), 0)
    member = route == patch
    before = jnp.sum(jnp.where(route < patch, 1.0, 0.0), axis=1, keepdims=True)
    room = CAP - jnp.sum(jnp.where(member, 1.0, 0.0), axis=1, keepdims=True)
    rank = jnp.sum(smaller, axis=0, keepdims=True) - jnp.sum(jnp.where(member, before, 0.0), axis=0, keepdims=True)
    room = jnp.sum(jnp.where(member, room, 0.0), axis=0, keepdims=True)
    base = (route << 8).astype(F32)
    ahead = base + ((cell * 3) >> 11).astype(F32) - rank
    most = jnp.full((8, rows), -1000.0, F32)
    for column, lead in zip(key_columns, columns_of(ahead)):
        for i in range(16):
            part = jnp.concatenate([column[8 * i:8 * i + 8]] * (rows // 128), axis=1)
            value = jnp.concatenate([lead[8 * i:8 * i + 8]] * (rows // 128), axis=1)
            most = jnp.where(part <= key, jnp.maximum(most, value), most)
    slot = (rank + jnp.minimum(jnp.max(most, axis=0, keepdims=True) - base, room)).astype(jnp.int32)
    return route * 32 + (slot & 31), slot >> 5


def stack_rows(spectra, third, cell):
    rows = spectra.shape[1]
    out = [jnp.where(third == q, spectra, 0.0) for q in range(3)]
    r = lax.broadcasted_iota(jnp.int32, (32, rows), 0)
    high = ((cell >> 8) + 1).astype(F32)
    low = (cell & 255).astype(F32)
    code = jnp.where((r & 4) == 0, high, low)
    out.append(jnp.where((r >> 3) == third, code, 0.0))
    return jnp.concatenate(out, axis=0).astype(BF)

def one_hot_rows(key):
    rows = key.shape[1]
    return jnp.where(lax.broadcasted_iota(jnp.int32, (1024, rows), 0) == key, 1.0, 0.0).astype(BF)

def write_messages(packed, turn, first, msg_ref):
    lane = lax.broadcasted_iota(jnp.int32, (32, 128), 1) >> 5
    for cb in range(2):
        groups = [packed[32 * g:32 * g + 32, 128 * cb:128 * cb + 128] for g in range(4)]
        for pm in range(4):
            out = jnp.zeros((32, 128), F32)
            for g in range(4):
                piece = groups[g]
                shift = (32 * (g - pm)) % 128
                if shift:
                    piece = pltpu.roll(piece, shift, 1)
                out = jnp.where(lane == g, piece, out)
            msg_ref[first + 4 * cb + pm] = pltpu.roll(out, turn, 1).astype(BF)


def regroup(msg_ref, sources, pair_ref):
    lane = lax.broadcasted_iota(jnp.int32, (32, 128), 1) >> 3
    lane8 = lane[:8]
    sub = lax.broadcasted_iota(jnp.int32, (8, 128), 0)
    msgs = [msg_ref[sources[t]].astype(F32) for t in range(16)]
    dense, codes = [], []
    for b in range(12):
        q = b // 4
        value, code = msgs[0], msgs[0][8 * q:8 * q + 8]
        for t in range(1, 16):
            value = jnp.where(lane == (b + t) % 16, msgs[t], value)
            code = jnp.where(lane8 == (12 + b % 4 + t) % 16, msgs[t][8 * q:8 * q + 8], code)
        dense.append(value)
        codes.append(pltpu.roll(code, 32 + 32 * q, 1))
    for f in range(8):
        tiles = []
        for pair in range(6):
            a = dense[2 * pair][8 * (f // 2):8 * (f // 2) + 8]
            b = dense[2 * pair + 1][8 * (f // 2):8 * (f // 2) + 8]
            if f % 2 == 0:
                b = pltpu.roll(b, 4, 0)
            else:
                a = pltpu.roll(a, 4, 0)
            tiles.append(jnp.where(sub < 4, a, b))
        pair_ref[f, 0:48, :] = jnp.concatenate(tiles, axis=0).astype(BF)
    out = []
    for cg in range(3):
        t = codes[4 * cg]
        for i in range(1, 4):
            t = jnp.where((sub & 3) == i, codes[4 * cg + i], t)
        out.append(t)
    out = jnp.concatenate(out, axis=0).astype(BF)
    for f in range(8):
        pair_ref[f, 48:72, :] = out
from jax.sharding import PartitionSpec as P
SIDE = 16
EPS = 1e-6
DAMPING = 0.1
STRETCH = 1.135235
CENTER = 0.99785729


def kernel_table():
    flat = np.arange(256)
    up, lo = flat // SIDE, flat % SIDE
    phase = (up[:, None] * up[None, :] + lo[:, None] * lo[None, :]) % SIDE
    angle = 2.0 * np.pi / SIDE * phase
    table = np.stack([np.cos(angle), -np.sin(angle)]) * STRETCH
    return table.astype(ml_dtypes.bfloat16).astype(np.float32)


TABLE_SCALE = 1.0 / (STRETCH * CENTER * SIDE) ** 2


WINDOW = 112


def bin_step(values, u, l, low, acc_ref):
    n = u.shape[1]
    iota_u = lax.broadcasted_iota(jnp.int32, (WINDOW, n), 0).astype(F32).astype(BF)
    iota_l = lax.broadcasted_iota(jnp.int32, (256, n), 0).astype(F32).astype(BF)
    one, zero = jnp.ones((), BF), jnp.zeros((), BF)
    start = pl.multiple_of(jnp.minimum(low, 256 - WINDOW), 8)
    mask = iota_u == jnp.where(u >= low.astype(F32), u - start.astype(F32), -1.0).astype(BF)
    parts = [jnp.where(mask, values[c:c + 1].astype(BF), zero) for c in range(4)] + [jnp.where(mask, one, zero)]
    hot = jnp.where(iota_l == l.astype(BF), one, zero)
    sums = lax.dot_general(jnp.concatenate(parts, axis=0), hot, NTD, preferred_element_type=F32)
    for c in range(5):
        acc_ref[c, pl.ds(start, WINDOW), :] += sums[WINDOW * c:WINDOW * c + WINDOW]


def spread(pair_ref, val_ref, code_ref):
    lane = lax.broadcasted_iota(jnp.int32, (8, 128), 1)
    first, last = jnp.zeros((8, 128), F32), jnp.zeros((8, 128), F32)
    lows, highs = [None] * 3, [None] * 3
    for half in range(2):
        for g in range(8):
            at = 128 * (8 * half + g)
            vals = pair_ref[half, g, 0:48, :].astype(F32)
            codes = pair_ref[half, g, 48:72, :].astype(F32)
            for cg in range(3):
                code = codes[8 * cg:8 * cg + 8]
                val_ref[cg, :, at:at + 128] = vals[16 * cg:16 * cg + 16]
                code_ref[cg, :, at:at + 128] = code
                low = jnp.where(code < 1.0, 999.0, code)
                lows[cg] = low if lows[cg] is None else jnp.minimum(lows[cg], low)
                highs[cg] = code if highs[cg] is None else jnp.maximum(highs[cg], code)
    for cg in range(3):
        first = jnp.where(lane == cg, jnp.min(lows[cg], axis=1, keepdims=True) - 1.0, first)
        last = jnp.where(lane == cg, jnp.max(highs[cg], axis=1, keepdims=True) - 1.0, last)
    return first.astype(jnp.int32), last.astype(jnp.int32)


def split(x):
    hi = x.astype(BF)
    return hi, (x - hi.astype(F32)).astype(BF)


def quad(a, b, c, d):
    return jnp.concatenate([jnp.concatenate([a, b], axis=1), jnp.concatenate([c, d], axis=1)], axis=0)


def swap(x):
    return quad(x[:256, :256], x[256:, :256], x[:256, 256:], x[256:, 256:])


def fit(acc_ref, w_ref, tab_ref, out_ref):
    kr, ki = tab_ref[0].astype(BF), tab_ref[1].astype(BF)
    plain, conj = quad(kr, -ki, ki, kr), quad(kr, ki, -ki, kr)
    dot = functools.partial(jnp.dot, preferred_element_type=F32)

    def left(x, m):
        return dot(jnp.concatenate([m, m], axis=1), jnp.concatenate(split(x), axis=0))

    def right(x, m):
        return dot(jnp.concatenate(split(x), axis=1), jnp.concatenate([m, m], axis=0))

    def forward(x):
        return swap(right(swap(left(x, plain)), conj))

    def inverse(x):
        return swap(right(swap(left(x, conj)), plain))

    def plane(f):
        return jnp.concatenate([w_ref[pl.ds(2 * h + f, 256, stride=4), :] for h in range(2)], axis=1)

    w0, w1 = plane(0) * TABLE_SCALE, plane(1) * TABLE_SCALE
    w = quad(w0, w1, w0, w1)
    lane = lax.broadcasted_iota(jnp.int32, (1, 512), 1)

    def total(x):
        s = jnp.sum(x, axis=0, keepdims=True)
        a = jnp.sum(s[:, :256], axis=1, keepdims=True)
        b = jnp.sum(s[:, 256:], axis=1, keepdims=True)
        return jnp.where(lane < 256, a, b)

    hits = acc_ref[4]
    hits = quad(hits, hits, hits, hits)
    field = quad(acc_ref[0], acc_ref[1], acc_ref[2], acc_ref[3])
    residual = w * forward(field)
    norm = total(residual * residual)
    g0 = inverse(w * residual)
    pulled = hits * g0
    alpha = norm / (total(pulled * g0) + DAMPING * norm + EPS)
    direction = residual
    residual = residual - alpha * (w * forward(pulled) + DAMPING * direction)
    new = total(residual * residual)
    direction = residual + (new / (norm + EPS)) * direction
    g1 = inverse(w * direction)
    beta = new / (total(hits * g1 * g1) + DAMPING * total(direction * direction) + EPS)
    model = alpha * g0 + beta * g1
    for part in range(2):
        for f in range(2):
            for h in range(2):
                out_ref[part, pl.ds(2 * h + f, 256, stride=4), :] = model[
                    256 * part:256 * part + 256, 256 * f + 128 * h:256 * f + 128 * h + 128]


def solve_kernel(pair_ref, w_hbm, tab_hbm, out_ref, acc_ref, w_ref, tab_ref, val_ref, code_ref, span_vm, span_sm, sems):
    fetch = [pltpu.make_async_copy(w_hbm, w_ref, sems.at[0]), pltpu.make_async_copy(tab_hbm, tab_ref, sems.at[1])]
    for copy in fetch:
        copy.start()
    span_vm[0], span_vm[1] = spread(pair_ref, val_ref, code_ref)
    spans = pltpu.make_async_copy(span_vm, span_sm, sems.at[2])
    spans.start()
    acc_ref[...] = jnp.zeros_like(acc_ref)
    spans.wait()

    @pl.loop(0, 3)
    def _(cg):
        for i in range(4):
            first, last = span_sm[0, i, cg], span_sm[1, i, cg]
            first = (first // 8) * 8
            wide = last - first
            count = sum((wide >= WINDOW * k).astype(jnp.int32) for k in range(-(-256 // WINDOW)))

            @pl.loop(0, count)
            def _(again):
                code = code_ref[cg]
                bin_step(val_ref[cg, 4 * i:4 * i + 4, :], code[i:i + 1] - 1.0, code[4 + i:5 + i], first + again * WINDOW, acc_ref)

    for copy in fetch:
        copy.wait()
    fit(acc_ref, w_ref, tab_ref, out_ref)


MESH_ID = pl.DeviceIdType.MESH


def peer_loop(n, me, body):
    lax.fori_loop(1, n, lambda i, carry: (body(lax.rem(me + i, n)), carry)[1], 0)


def exchange_kernel(bins_ref, traces_ref, route_ref, cell_ref, out_ref,
                    traces_vm, hot_vm, bins_vm, msg_out, msg_in, pair_out,
                    trace_sem, own_sem, bin_send, bin_recv, msg_send, msg_recv, pair_send, pair_recv):
    me_p, me_f = lax.axis_index("patch"), lax.axis_index("freq")
    me_x, me_z = me_p // 8, lax.rem(me_p, 8)
    barrier = pltpu.get_barrier_semaphore()
    peer_loop(8, me_f, lambda f: pl.semaphore_signal(barrier, inc=1, device_id={"freq": f}, device_id_type=MESH_ID))
    peer_loop(32, me_p, lambda p: pl.semaphore_signal(barrier, inc=1, device_id={"patch": p}, device_id_type=MESH_ID))
    fetch = pltpu.make_async_copy(traces_ref, traces_vm, trace_sem)
    fetch.start()
    sub = lax.broadcasted_iota(jnp.int32, (8, 128), 0)
    bins_vm[me_f] = jnp.where((sub & 1) == 1, bins_ref[1], bins_ref[0])

    def bin_copy(f, slot):
        return pltpu.make_async_remote_copy(
            src_ref=bins_vm.at[me_f], dst_ref=bins_vm.at[slot], send_sem=bin_send.at[f],
            recv_sem=bin_recv.at[slot], device_id={"freq": f}, device_id_type=MESH_ID)

    def msg_copy(p, slot):
        return pltpu.make_async_remote_copy(
            src_ref=msg_out.at[p], dst_ref=msg_in.at[slot], send_sem=msg_send.at[p],
            recv_sem=msg_recv.at[slot], device_id={"patch": p}, device_id_type=MESH_ID)

    def pair_copy(half, f, slot):
        return pltpu.make_async_remote_copy(
            src_ref=pair_out.at[half, f], dst_ref=out_ref.at[half, slot], send_sem=pair_send.at[half, f],
            recv_sem=pair_recv.at[half, slot], device_id={"freq": f}, device_id_type=MESH_ID)

    def own_copy(half):
        return pltpu.make_async_copy(pair_out.at[half, me_f], out_ref.at[half, me_f], own_sem.at[half])

    pl.semaphore_wait(barrier, 38)
    peer_loop(8, me_f, lambda f: bin_copy(f, me_f).start())
    key, third = routing(route_ref[...], cell_ref[...])
    hot_vm[...] = one_hot_rows(key)
    peer_loop(8, me_f, lambda f: bin_copy(f, f).wait_recv())
    basis = make_basis(bins_vm, traces_vm.shape[1])
    fetch.wait()
    spectra = lax.dot_general(basis, traces_vm[...], NTD, preferred_element_type=F32)
    stacked = stack_rows(spectra, third, cell_ref[...])
    order = [(i // 8, i % 8) for i in range(32)]
    targets = [lax.rem(me_x + dx, 4) * 8 + lax.rem(me_z + dz, 8) for dx, dz in order]
    sources = [lax.rem(me_x + 4 - dx, 4) * 8 + lax.rem(me_z + 8 - dz, 8) for dx, dz in order]
    for dx in range(4):
        plane = lax.rem(me_x + dx, 4)
        packed = lax.dot_general(stacked, hot_vm[pl.ds(pl.multiple_of(256 * plane, 256), 256), :], NTD, preferred_element_type=F32)
        write_messages(packed, 8 * lax.rem(me_p, 16), 8 * plane, msg_out)
        for p in targets[max(1, 8 * dx):8 * dx + 8]:
            msg_copy(p, me_p).start()
    msg_in[me_p] = msg_out[me_p]
    for half in range(2):
        for p in sources[max(1, 16 * half):16 * half + 16]:
            msg_copy(p, p).wait_recv()
        first = lax.rem(me_x + 2 * half, 4)
        second = lax.rem(me_x + 2 * half + 3, 4)
        is_odd = lax.rem(me_x, 2)
        planes = (first + is_odd * (second - first), second + is_odd * (first - second))
        regroup(msg_in, [planes[t // 8] * 8 + t % 8 for t in range(16)], pair_out.at[half])
        peer_loop(8, me_f, lambda f: pair_copy(half, f, me_f).start())
        own_copy(half).start()
    peer_loop(8, me_f, lambda f: bin_copy(f, me_f).wait_send())
    for p in targets[1:]:
        msg_copy(p, me_p).wait_send()
    for half in range(2):
        own_copy(half).wait()
        peer_loop(8, me_f, lambda f: pair_copy(half, f, f).wait_recv())
        peer_loop(8, me_f, lambda f: pair_copy(half, f, me_f).wait_send())

def on_device(traces, routes, cells, band_bins, spectral_weight):
    rows = traces.shape[0]
    vm = pl.BlockSpec(memory_space=pltpu.VMEM)
    sm = pl.BlockSpec(memory_space=pltpu.SMEM)
    anywhere = pl.BlockSpec(memory_space=pl.ANY)
    dma = pltpu.SemaphoreType.DMA
    both = pl.pallas_call(
        exchange_kernel,
        out_shape=jax.ShapeDtypeStruct((2, 8, 72, 128), BF),
        in_specs=[sm, anywhere, vm, vm],
        out_specs=anywhere,
        scratch_shapes=[
            pltpu.VMEM(traces.shape, BF), pltpu.VMEM((1024, rows), BF), pltpu.VMEM((8, 8, 128), jnp.int32),
            pltpu.VMEM((32, 32, 128), BF), pltpu.VMEM((32, 32, 128), BF), pltpu.VMEM((2, 8, 72, 128), BF),
            dma, dma((2,)), dma((8,)), dma((8,)), dma((32,)), dma((32,)), dma((2, 8)), dma((2, 8)),
        ],
        compiler_params=pltpu.CompilerParams(
            collective_id=0, has_side_effects=True, vmem_limit_bytes=62 * 1024 * 1024),
        name="exchange",
    )(band_bins, traces, routes.reshape(1, rows), cells.reshape(1, rows))
    weight = spectral_weight.reshape(2, 512, 128).transpose(1, 0, 2).reshape(1024, 128)
    out = pl.pallas_call(
        solve_kernel,
        out_shape=jax.ShapeDtypeStruct((2, 1024, 128), F32),
        in_specs=[vm, anywhere, anywhere], out_specs=vm,
        scratch_shapes=[
            pltpu.VMEM((5, 256, 256), F32), pltpu.VMEM((1024, 128), F32), pltpu.VMEM((2, 256, 256), F32),
            pltpu.VMEM((3, 16, 2048), F32), pltpu.VMEM((3, 8, 2048), F32),
            pltpu.VMEM((2, 8, 128), jnp.int32), pltpu.SMEM((2, 8, 128), jnp.int32), dma((3,)),
        ],
        compiler_params=pltpu.CompilerParams(vmem_limit_bytes=60 * 1024 * 1024),
        name="solve",
    )(both, weight, jnp.asarray(kernel_table()))
    return out.reshape(2, 512, 2, 128).transpose(0, 2, 1, 3).reshape(2, 2, 65536)


def solution(mesh):
    return jax.shard_map(
        on_device,
        mesh=mesh,
        in_specs=(P(("patch", "freq"), None), P(("patch", "freq"), None), P(("patch", "freq")), P("freq"), P("freq", "patch")),
        out_specs=P(None, "freq", "patch"),
        check_vma=False,
    )
```

```python
import functools, math
import jax
import jax.numpy as jnp
import ml_dtypes
import numpy as np
from jax import lax
from jax.experimental import pallas as pl
from jax.experimental.pallas import tpu as pltpu
F32 = jnp.float32
BF = jnp.bfloat16
CAP = 96
NTD=(((1,),(1,)),((),()))


def cosine(phase, n):
    quad = (phase + n // 8) // (n // 4)
    rest = (phase - quad * (n // 4)).astype(F32) * (2.0 * math.pi / n)
    sq = rest * rest
    c = 1.0 + sq * (-0.5 + sq * (1.0/24 + sq * (-1.0/720 + sq * (1.0/40320))))
    s = rest * (1.0 + sq * (-1.0/6 + sq * (1.0/120 + sq * (-1.0/5040))))
    odd = (quad & 1) == 1
    val = jnp.where(odd, s, c)
    neg = ((quad + 1) & 2) == 2
    return jnp.where(neg, -val, val)

def make_basis(bins_ref, nt):
    sub = lax.broadcasted_iota(jnp.int32, (8, 128), 0)
    k = jnp.concatenate([jnp.where(sub < 4, bins_ref[2 * i], bins_ref[2 * i + 1]) for i in range(4)], axis=0)
    part = (lax.broadcasted_iota(jnp.int32, (32, 128), 0) // 2) & 1
    t = lax.broadcasted_iota(jnp.int32, (32, nt), 1)
    kk = jnp.concatenate([k] * (nt // 128), axis=1)
    pp = jnp.concatenate([part * (nt // 4)] * (nt // 128), axis=1)
    phase = (kk * t + pp) & (nt - 1)
    return (cosine(phase, nt) * (1.0 / math.sqrt(nt))).astype(BF)

def columns_of(row):
    return [jnp.broadcast_to(row[:, a:a + 128], (128, 128)).T for a in range(0, row.shape[1], 128)]


def routing(route, cell):
    rows = route.shape[1]
    key = (route << 26) + (cell << 10) + lax.broadcasted_iota(jnp.int32, (1, rows), 1)
    key_columns = columns_of(key)
    smaller = jnp.zeros((8, rows), F32)
    for column in key_columns:
        for i in range(16):
            part = jnp.concatenate([column[8 * i:8 * i + 8]] * (rows // 128), axis=1)
            smaller = smaller + jnp.where(part < key, 1.0, 0.0)
    patch = lax.broadcasted_iota(jnp.int32, (32, rows), 0)
    member = route == patch
    before = jnp.sum(jnp.where(route < patch, 1.0, 0.0), axis=1, keepdims=True)
    room = CAP - jnp.sum(jnp.where(member, 1.0, 0.0), axis=1, keepdims=True)
    rank = jnp.sum(smaller, axis=0, keepdims=True) - jnp.sum(jnp.where(member, before, 0.0), axis=0, keepdims=True)
    room = jnp.sum(jnp.where(member, room, 0.0), axis=0, keepdims=True)
    base = (route << 8).astype(F32)
    ahead = base + ((cell * 3) >> 11).astype(F32) - rank
    most = jnp.full((8, rows), -1000.0, F32)
    for column, lead in zip(key_columns, columns_of(ahead)):
        for i in range(16):
            part = jnp.concatenate([column[8 * i:8 * i + 8]] * (rows // 128), axis=1)
            value = jnp.concatenate([lead[8 * i:8 * i + 8]] * (rows // 128), axis=1)
            most = jnp.where(part <= key, jnp.maximum(most, value), most)
    slot = (rank + jnp.minimum(jnp.max(most, axis=0, keepdims=True) - base, room)).astype(jnp.int32)
    return route * 32 + (slot & 31), slot >> 5


def stack_rows(spectra, third, cell):
    rows = spectra.shape[1]
    out = [jnp.where(third == q, spectra, 0.0) for q in range(3)]
    r = lax.broadcasted_iota(jnp.int32, (32, rows), 0)
    high = ((cell >> 8) + 1).astype(F32)
    low = (cell & 255).astype(F32)
    code = jnp.where((r & 4) == 0, high, low)
    out.append(jnp.where((r >> 3) == third, code, 0.0))
    return jnp.concatenate(out, axis=0).astype(BF)

def one_hot_rows(key):
    rows = key.shape[1]
    return jnp.where(lax.broadcasted_iota(jnp.int32, (1024, rows), 0) == key, 1.0, 0.0).astype(BF)

def write_messages(packed, turn, first, msg_ref):
    lane = lax.broadcasted_iota(jnp.int32, (32, 128), 1) >> 5
    for cb in range(2):
        groups = [packed[32 * g:32 * g + 32, 128 * cb:128 * cb + 128] for g in range(4)]
        for pm in range(4):
            out = jnp.zeros((32, 128), F32)
            for g in range(4):
                piece = groups[g]
                shift = (32 * (g - pm)) % 128
                if shift:
                    piece = pltpu.roll(piece, shift, 1)
                out = jnp.where(lane == g, piece, out)
            msg_ref[first + 4 * cb + pm] = pltpu.roll(out, turn, 1).astype(BF)


def regroup(msg_ref, sources, pair_ref):
    lane = lax.broadcasted_iota(jnp.int32, (32, 128), 1) >> 3
    lane8 = lane[:8]
    sub = lax.broadcasted_iota(jnp.int32, (8, 128), 0)
    msgs = [msg_ref[sources[t]].astype(F32) for t in range(16)]
    dense, codes = [], []
    for b in range(12):
        q = b // 4
        value, code = msgs[0], msgs[0][8 * q:8 * q + 8]
        for t in range(1, 16):
            value = jnp.where(lane == (b + t) % 16, msgs[t], value)
            code = jnp.where(lane8 == (12 + b % 4 + t) % 16, msgs[t][8 * q:8 * q + 8], code)
        dense.append(value)
        codes.append(pltpu.roll(code, 32 + 32 * q, 1))
    for f in range(8):
        tiles = []
        for pair in range(6):
            a = dense[2 * pair][8 * (f // 2):8 * (f // 2) + 8]
            b = dense[2 * pair + 1][8 * (f // 2):8 * (f // 2) + 8]
            if f % 2 == 0:
                b = pltpu.roll(b, 4, 0)
            else:
                a = pltpu.roll(a, 4, 0)
            tiles.append(jnp.where(sub < 4, a, b))
        pair_ref[f, 0:48, :] = jnp.concatenate(tiles, axis=0).astype(BF)
    out = []
    for cg in range(3):
        t = codes[4 * cg]
        for i in range(1, 4):
            t = jnp.where((sub & 3) == i, codes[4 * cg + i], t)
        out.append(t)
    out = jnp.concatenate(out, axis=0).astype(BF)
    for f in range(8):
        pair_ref[f, 48:72, :] = out
from jax.sharding import PartitionSpec as P
SIDE = 16
EPS = 1e-6
DAMPING = 0.1
STRETCH = 1.135235
CENTER = 0.99785729


def kernel_table():
    flat = np.arange(256)
    up, lo = flat // SIDE, flat % SIDE
    phase = (up[:, None] * up[None, :] + lo[:, None] * lo[None, :]) % SIDE
    angle = 2.0 * np.pi / SIDE * phase
    table = np.stack([np.cos(angle), -np.sin(angle)]) * STRETCH
    return table.astype(ml_dtypes.bfloat16).astype(np.float32)


TABLE_SCALE = 1.0 / (STRETCH * CENTER * SIDE) ** 2


WINDOW = 112
USUAL = ((64, 88, 96, 112), (112, 120, 112, 112), (104, 96, 80, 64))


def bin_step(values, u, l, low, window, acc_ref):
    n = u.shape[1]
    iota_u = lax.broadcasted_iota(jnp.int32, (window, n), 0).astype(F32).astype(BF)
    iota_l = lax.broadcasted_iota(jnp.int32, (256, n), 0).astype(F32).astype(BF)
    one, zero = jnp.ones((), BF), jnp.zeros((), BF)
    start = pl.multiple_of(jnp.minimum(low, 256 - window), 8)
    mask = iota_u == jnp.where(u >= low.astype(F32), u - start.astype(F32), -1.0).astype(BF)
    parts = [jnp.where(mask, values[c:c + 1].astype(BF), zero) for c in range(4)] + [jnp.where(mask, one, zero)]
    hot = jnp.where(iota_l == l.astype(BF), one, zero)
    sums = lax.dot_general(jnp.concatenate(parts, axis=0), hot, NTD, preferred_element_type=F32)
    for c in range(5):
        acc_ref[c, pl.ds(start, window), :] += sums[window * c:window * c + window]


def spread(pair_ref, val_ref, code_ref):
    lane = lax.broadcasted_iota(jnp.int32, (8, 128), 1)
    first, last = jnp.zeros((8, 128), F32), jnp.zeros((8, 128), F32)
    lows, highs = [None] * 3, [None] * 3
    for half in range(2):
        for g in range(8):
            at = 128 * (8 * half + g)
            vals = pair_ref[half, g, 0:48, :].astype(F32)
            codes = pair_ref[half, g, 48:72, :].astype(F32)
            for cg in range(3):
                code = codes[8 * cg:8 * cg + 8]
                val_ref[cg, :, at:at + 128] = vals[16 * cg:16 * cg + 16]
                code_ref[cg, :, at:at + 128] = code
                low = jnp.where(code < 1.0, 999.0, code)
                lows[cg] = low if lows[cg] is None else jnp.minimum(lows[cg], low)
                highs[cg] = code if highs[cg] is None else jnp.maximum(highs[cg], code)
    for cg in range(3):
        first = jnp.where(lane == cg, jnp.min(lows[cg], axis=1, keepdims=True) - 1.0, first)
        last = jnp.where(lane == cg, jnp.max(highs[cg], axis=1, keepdims=True) - 1.0, last)
    return first.astype(jnp.int32), last.astype(jnp.int32)


def split(x):
    hi = x.astype(BF)
    return hi, (x - hi.astype(F32)).astype(BF)


def quad(a, b, c, d):
    return jnp.concatenate([jnp.concatenate([a, b], axis=1), jnp.concatenate([c, d], axis=1)], axis=0)


def swap(x):
    return quad(x[:256, :256], x[256:, :256], x[:256, 256:], x[256:, 256:])


def fit(acc_ref, w_ref, tab_ref, out_ref):
    kr, ki = tab_ref[0].astype(BF), tab_ref[1].astype(BF)
    plain, conj = quad(kr, -ki, ki, kr), quad(kr, ki, -ki, kr)
    dot = functools.partial(jnp.dot, preferred_element_type=F32)

    def left(x, m):
        return dot(jnp.concatenate([m, m], axis=1), jnp.concatenate(split(x), axis=0))

    def right(x, m):
        return dot(jnp.concatenate(split(x), axis=1), jnp.concatenate([m, m], axis=0))

    def forward(x):
        return swap(right(swap(left(x, plain)), conj))

    def inverse(x):
        return swap(right(swap(left(x, conj)), plain))

    def plane(f):
        return jnp.concatenate([w_ref[pl.ds(2 * h + f, 256, stride=4), :] for h in range(2)], axis=1)

    w0, w1 = plane(0) * TABLE_SCALE, plane(1) * TABLE_SCALE
    w = quad(w0, w1, w0, w1)
    lane = lax.broadcasted_iota(jnp.int32, (1, 512), 1)

    def total(x):
        s = jnp.sum(x, axis=0, keepdims=True)
        a = jnp.sum(s[:, :256], axis=1, keepdims=True)
        b = jnp.sum(s[:, 256:], axis=1, keepdims=True)
        return jnp.where(lane < 256, a, b)

    hits = acc_ref[4]
    hits = quad(hits, hits, hits, hits)
    field = quad(acc_ref[0], acc_ref[1], acc_ref[2], acc_ref[3])
    residual = w * forward(field)
    norm = total(residual * residual)
    g0 = inverse(w * residual)
    pulled = hits * g0
    alpha = norm / (total(pulled * g0) + DAMPING * norm + EPS)
    direction = residual
    residual = residual - alpha * (w * forward(pulled) + DAMPING * direction)
    new = total(residual * residual)
    direction = residual + (new / (norm + EPS)) * direction
    g1 = swap(dot(swap(dot(conj, (w * direction).astype(BF))).astype(BF), plain))
    beta = new / (total(hits * g1 * g1) + DAMPING * total(direction * direction) + EPS)
    model = alpha * g0 + beta * g1
    for part in range(2):
        for f in range(2):
            for h in range(2):
                out_ref[part, pl.ds(2 * h + f, 256, stride=4), :] = model[
                    256 * part:256 * part + 256, 256 * f + 128 * h:256 * f + 128 * h + 128]


def solve_kernel(pair_ref, w_hbm, tab_hbm, out_ref, acc_ref, w_ref, tab_ref, val_ref, code_ref, span_vm, span_sm, sems):
    fetch = [pltpu.make_async_copy(w_hbm, w_ref, sems.at[0]), pltpu.make_async_copy(tab_hbm, tab_ref, sems.at[1])]
    for copy in fetch:
        copy.start()
    span_vm[0], span_vm[1] = spread(pair_ref, val_ref, code_ref)
    spans = pltpu.make_async_copy(span_vm, span_sm, sems.at[2])
    spans.start()
    acc_ref[...] = jnp.zeros_like(acc_ref)
    spans.wait()

    for cg in range(3):
        steps, usual = [], True
        for i in range(4):
            first, last = span_sm[0, i, cg], span_sm[1, i, cg]
            first = jnp.minimum((first // 8) * 8, 248)
            wide = last - first
            usual = jnp.logical_and(usual, wide < USUAL[cg][i])
            steps.append((first, sum((wide >= WINDOW * k).astype(jnp.int32) for k in range(-(-256 // WINDOW)))))

        def add(i, low, window):
            code = code_ref[cg]
            bin_step(val_ref[cg, 4 * i:4 * i + 4, :], code[i:i + 1] - 1.0, code[4 + i:5 + i], low, window, acc_ref)

        @pl.when(usual)
        def _():
            for i in range(4):
                add(i, steps[i][0], USUAL[cg][i])

        @pl.when(jnp.logical_not(usual))
        def _():
            for i in range(4):
                pl.loop(0, steps[i][1])(lambda again: add(i, steps[i][0] + again * WINDOW, WINDOW))

    for copy in fetch:
        copy.wait()
    fit(acc_ref, w_ref, tab_ref, out_ref)


MESH_ID = pl.DeviceIdType.MESH


def peer_loop(n, me, body):
    lax.fori_loop(1, n, lambda i, carry: (body(lax.rem(me + i, n)), carry)[1], 0)


def exchange_kernel(bins_ref, traces_ref, route_ref, cell_ref, out_ref,
                    traces_vm, hot_vm, bins_vm, msg_out, msg_in, pair_out,
                    trace_sem, own_sem, bin_send, bin_recv, msg_send, msg_recv, pair_send, pair_recv):
    me_p, me_f = lax.axis_index("patch"), lax.axis_index("freq")
    me_x, me_z = me_p // 8, lax.rem(me_p, 8)
    barrier = pltpu.get_barrier_semaphore()
    peer_loop(8, me_f, lambda f: pl.semaphore_signal(barrier, inc=1, device_id={"freq": f}, device_id_type=MESH_ID))
    peer_loop(32, me_p, lambda p: pl.semaphore_signal(barrier, inc=1, device_id={"patch": p}, device_id_type=MESH_ID))
    fetch = pltpu.make_async_copy(traces_ref, traces_vm, trace_sem)
    fetch.start()
    sub = lax.broadcasted_iota(jnp.int32, (8, 128), 0)
    bins_vm[me_f] = jnp.where((sub & 1) == 1, bins_ref[1], bins_ref[0])

    def bin_copy(f, slot):
        return pltpu.make_async_remote_copy(
            src_ref=bins_vm.at[me_f], dst_ref=bins_vm.at[slot], send_sem=bin_send.at[f],
            recv_sem=bin_recv.at[slot], device_id={"freq": f}, device_id_type=MESH_ID)

    def msg_copy(p, slot):
        return pltpu.make_async_remote_copy(
            src_ref=msg_out.at[p], dst_ref=msg_in.at[slot], send_sem=msg_send.at[p],
            recv_sem=msg_recv.at[slot], device_id={"patch": p}, device_id_type=MESH_ID)

    def pair_copy(half, f, slot):
        return pltpu.make_async_remote_copy(
            src_ref=pair_out.at[half, f], dst_ref=out_ref.at[half, slot], send_sem=pair_send.at[half, f],
            recv_sem=pair_recv.at[half, slot], device_id={"freq": f}, device_id_type=MESH_ID)

    def own_copy(half):
        return pltpu.make_async_copy(pair_out.at[half, me_f], out_ref.at[half, me_f], own_sem.at[half])

    pl.semaphore_wait(barrier, 38)
    peer_loop(8, me_f, lambda f: bin_copy(f, me_f).start())
    key, third = routing(route_ref[...], cell_ref[...])
    hot_vm[...] = one_hot_rows(key)
    peer_loop(8, me_f, lambda f: bin_copy(f, f).wait_recv())
    basis = make_basis(bins_vm, traces_vm.shape[1])
    fetch.wait()
    spectra = lax.dot_general(basis, traces_vm[...], NTD, preferred_element_type=F32)
    stacked = stack_rows(spectra, third, cell_ref[...])
    order = [(i // 8, i % 8) for i in range(32)]
    targets = [lax.rem(me_x + dx, 4) * 8 + lax.rem(me_z + dz, 8) for dx, dz in order]
    sources = [lax.rem(me_x + 4 - dx, 4) * 8 + lax.rem(me_z + 8 - dz, 8) for dx, dz in order]
    for dx in range(4):
        plane = lax.rem(me_x + dx, 4)
        packed = lax.dot_general(stacked, hot_vm[pl.ds(pl.multiple_of(256 * plane, 256), 256), :], NTD, preferred_element_type=F32)
        write_messages(packed, 8 * lax.rem(me_p, 16), 8 * plane, msg_out)
        for p in targets[max(1, 8 * dx):8 * dx + 8]:
            msg_copy(p, me_p).start()
    msg_in[me_p] = msg_out[me_p]
    for half in range(2):
        for p in sources[max(1, 16 * half):16 * half + 16]:
            msg_copy(p, p).wait_recv()
        first = lax.rem(me_x + 2 * half, 4)
        second = lax.rem(me_x + 2 * half + 3, 4)
        is_odd = lax.rem(me_x, 2)
        planes = (first + is_odd * (second - first), second + is_odd * (first - second))
        regroup(msg_in, [planes[t // 8] * 8 + t % 8 for t in range(16)], pair_out.at[half])
        peer_loop(8, me_f, lambda f: pair_copy(half, f, me_f).start())
        own_copy(half).start()
    peer_loop(8, me_f, lambda f: bin_copy(f, me_f).wait_send())
    for p in targets[1:]:
        msg_copy(p, me_p).wait_send()
    for half in range(2):
        own_copy(half).wait()
        peer_loop(8, me_f, lambda f: pair_copy(half, f, f).wait_recv())
        peer_loop(8, me_f, lambda f: pair_copy(half, f, me_f).wait_send())

def on_device(traces, routes, cells, band_bins, spectral_weight):
    rows = traces.shape[0]
    vm = pl.BlockSpec(memory_space=pltpu.VMEM)
    sm = pl.BlockSpec(memory_space=pltpu.SMEM)
    anywhere = pl.BlockSpec(memory_space=pl.ANY)
    dma = pltpu.SemaphoreType.DMA
    both = pl.pallas_call(
        exchange_kernel,
        out_shape=jax.ShapeDtypeStruct((2, 8, 72, 128), BF),
        in_specs=[sm, anywhere, vm, vm],
        out_specs=anywhere,
        scratch_shapes=[
            pltpu.VMEM(traces.shape, BF), pltpu.VMEM((1024, rows), BF), pltpu.VMEM((8, 8, 128), jnp.int32),
            pltpu.VMEM((32, 32, 128), BF), pltpu.VMEM((32, 32, 128), BF), pltpu.VMEM((2, 8, 72, 128), BF),
            dma, dma((2,)), dma((8,)), dma((8,)), dma((32,)), dma((32,)), dma((2, 8)), dma((2, 8)),
        ],
        compiler_params=pltpu.CompilerParams(
            collective_id=0, has_side_effects=True, vmem_limit_bytes=62 * 1024 * 1024),
        name="exchange",
    )(band_bins, traces, routes.reshape(1, rows), cells.reshape(1, rows))
    weight = spectral_weight.reshape(2, 512, 128).transpose(1, 0, 2).reshape(1024, 128)
    out = pl.pallas_call(
        solve_kernel,
        out_shape=jax.ShapeDtypeStruct((2, 1024, 128), F32),
        in_specs=[vm, anywhere, anywhere], out_specs=vm,
        scratch_shapes=[
            pltpu.VMEM((5, 256, 256), F32), pltpu.VMEM((1024, 128), F32), pltpu.VMEM((2, 256, 256), F32),
            pltpu.VMEM((3, 16, 2048), F32), pltpu.VMEM((3, 8, 2048), F32),
            pltpu.VMEM((2, 8, 128), jnp.int32), pltpu.SMEM((2, 8, 128), jnp.int32), dma((3,)),
        ],
        compiler_params=pltpu.CompilerParams(vmem_limit_bytes=60 * 1024 * 1024),
        name="solve",
    )(both, weight, jnp.asarray(kernel_table()))
    return out.reshape(2, 512, 2, 128).transpose(0, 2, 1, 3).reshape(2, 2, 65536)


def solution(mesh):
    return jax.shard_map(
        on_device,
        mesh=mesh,
        in_specs=(P(("patch", "freq"), None), P(("patch", "freq"), None), P(("patch", "freq")), P("freq"), P("freq", "patch")),
        out_specs=P(None, "freq", "patch"),
        check_vma=False,
    )
```

```python
import functools, math
import jax
import jax.numpy as jnp
import ml_dtypes
import numpy as np
from jax import lax
from jax.experimental import pallas as pl
from jax.experimental.pallas import tpu as pltpu
F32 = jnp.float32
BF = jnp.bfloat16
CAP = 96
NTD=(((1,),(1,)),((),()))


def cosine(phase, n):
    quad = (phase + n // 8) // (n // 4)
    rest = (phase - quad * (n // 4)).astype(F32) * (2.0 * math.pi / n)
    sq = rest * rest
    c = 1.0 + sq * (-0.5 + sq * (1.0/24 + sq * (-1.0/720 + sq * (1.0/40320))))
    s = rest * (1.0 + sq * (-1.0/6 + sq * (1.0/120 + sq * (-1.0/5040))))
    odd = (quad & 1) == 1
    val = jnp.where(odd, s, c)
    neg = ((quad + 1) & 2) == 2
    return jnp.where(neg, -val, val)

def make_basis(bins_ref, nt):
    sub = lax.broadcasted_iota(jnp.int32, (8, 128), 0)
    k = jnp.concatenate([jnp.where(sub < 4, bins_ref[2 * i], bins_ref[2 * i + 1]) for i in range(4)], axis=0)
    part = (lax.broadcasted_iota(jnp.int32, (32, 128), 0) // 2) & 1
    t = lax.broadcasted_iota(jnp.int32, (32, nt), 1)
    kk = jnp.concatenate([k] * (nt // 128), axis=1)
    pp = jnp.concatenate([part * (nt // 4)] * (nt // 128), axis=1)
    phase = (kk * t + pp) & (nt - 1)
    return (cosine(phase, nt) * (1.0 / math.sqrt(nt))).astype(BF)

def columns_of(row):
    return [jnp.broadcast_to(row[:, a:a + 128], (128, 128)).T for a in range(0, row.shape[1], 128)]


def routing(route, cell):
    rows = route.shape[1]
    key = (route << 26) + (cell << 10) + lax.broadcasted_iota(jnp.int32, (1, rows), 1)
    key_columns = columns_of(key)
    smaller = jnp.zeros((8, rows), F32)
    for column in key_columns:
        for i in range(16):
            part = jnp.concatenate([column[8 * i:8 * i + 8]] * (rows // 128), axis=1)
            smaller = smaller + jnp.where(part < key, 1.0, 0.0)
    patch = lax.broadcasted_iota(jnp.int32, (32, rows), 0)
    member = route == patch
    before = jnp.sum(jnp.where(route < patch, 1.0, 0.0), axis=1, keepdims=True)
    room = CAP - jnp.sum(jnp.where(member, 1.0, 0.0), axis=1, keepdims=True)
    rank = jnp.sum(smaller, axis=0, keepdims=True) - jnp.sum(jnp.where(member, before, 0.0), axis=0, keepdims=True)
    room = jnp.sum(jnp.where(member, room, 0.0), axis=0, keepdims=True)
    base = (route << 8).astype(F32)
    ahead = base + ((cell * 3) >> 11).astype(F32) - rank
    most = jnp.full((8, rows), -1000.0, F32)
    for column, lead in zip(key_columns, columns_of(ahead)):
        for i in range(16):
            part = jnp.concatenate([column[8 * i:8 * i + 8]] * (rows // 128), axis=1)
            value = jnp.concatenate([lead[8 * i:8 * i + 8]] * (rows // 128), axis=1)
            most = jnp.where(part <= key, jnp.maximum(most, value), most)
    slot = (rank + jnp.minimum(jnp.max(most, axis=0, keepdims=True) - base, room)).astype(jnp.int32)
    return route * 32 + (slot & 31), slot >> 5


def stack_rows(spectra, third, cell):
    rows = spectra.shape[1]
    out = [jnp.where(third == q, spectra, 0.0) for q in range(3)]
    r = lax.broadcasted_iota(jnp.int32, (32, rows), 0)
    high = ((cell >> 8) + 1).astype(F32)
    low = (cell & 255).astype(F32)
    code = jnp.where((r & 4) == 0, high, low)
    out.append(jnp.where((r >> 3) == third, code, 0.0))
    return jnp.concatenate(out, axis=0).astype(BF)

def one_hot_rows(key):
    rows = key.shape[1]
    return jnp.where(lax.broadcasted_iota(jnp.int32, (1024, rows), 0) == key, 1.0, 0.0).astype(BF)

def write_messages(packed, turn, first, msg_ref):
    lane = lax.broadcasted_iota(jnp.int32, (32, 128), 1) >> 5
    for cb in range(2):
        groups = [packed[32 * g:32 * g + 32, 128 * cb:128 * cb + 128] for g in range(4)]
        for pm in range(4):
            out = jnp.zeros((32, 128), F32)
            for g in range(4):
                piece = groups[g]
                shift = (32 * (g - pm)) % 128
                if shift:
                    piece = pltpu.roll(piece, shift, 1)
                out = jnp.where(lane == g, piece, out)
            msg_ref[first + 4 * cb + pm] = pltpu.roll(out, turn, 1).astype(BF)


def regroup(msg_ref, sources, pair_ref):
    lane = lax.broadcasted_iota(jnp.int32, (32, 128), 1) >> 3
    lane8 = lane[:8]
    sub = lax.broadcasted_iota(jnp.int32, (8, 128), 0)
    msgs = [msg_ref[sources[t]].astype(F32) for t in range(16)]
    dense, codes = [], []
    for b in range(12):
        q = b // 4
        value, code = msgs[0], msgs[0][8 * q:8 * q + 8]
        for t in range(1, 16):
            value = jnp.where(lane == (b + t) % 16, msgs[t], value)
            code = jnp.where(lane8 == (12 + b % 4 + t) % 16, msgs[t][8 * q:8 * q + 8], code)
        dense.append(value)
        codes.append(pltpu.roll(code, 32 + 32 * q, 1))
    for f in range(8):
        tiles = []
        for pair in range(6):
            a = dense[2 * pair][8 * (f // 2):8 * (f // 2) + 8]
            b = dense[2 * pair + 1][8 * (f // 2):8 * (f // 2) + 8]
            if f % 2 == 0:
                b = pltpu.roll(b, 4, 0)
            else:
                a = pltpu.roll(a, 4, 0)
            tiles.append(jnp.where(sub < 4, a, b))
        pair_ref[f, 0:48, :] = jnp.concatenate(tiles, axis=0).astype(BF)
    out = []
    for cg in range(3):
        t = codes[4 * cg]
        for i in range(1, 4):
            t = jnp.where((sub & 3) == i, codes[4 * cg + i], t)
        out.append(t)
    out = jnp.concatenate(out, axis=0).astype(BF)
    for f in range(8):
        pair_ref[f, 48:72, :] = out
from jax.sharding import PartitionSpec as P
SIDE = 16
EPS = 1e-6
DAMPING = 0.1
STRETCH = 1.135235
CENTER = 0.99785729


def kernel_table():
    flat = np.arange(256)
    up, lo = flat // SIDE, flat % SIDE
    phase = (up[:, None] * up[None, :] + lo[:, None] * lo[None, :]) % SIDE
    angle = 2.0 * np.pi / SIDE * phase
    table = np.stack([np.cos(angle), -np.sin(angle)]) * STRETCH
    return table.astype(ml_dtypes.bfloat16).astype(np.float32)


TABLE_SCALE = 1.0 / (STRETCH * CENTER * SIDE) ** 2


WINDOW = 112
USUAL = ((64, 88, 96, 112), (112, 120, 112, 112), (104, 96, 80, 64))


def bin_step(values, u, l, low, window, acc_ref):
    n = u.shape[1]
    iota_u = lax.broadcasted_iota(jnp.int32, (window, n), 0).astype(F32).astype(BF)
    iota_l = lax.broadcasted_iota(jnp.int32, (256, n), 0).astype(F32).astype(BF)
    one, zero = jnp.ones((), BF), jnp.zeros((), BF)
    start = pl.multiple_of(jnp.minimum(low, 256 - window), 8)
    mask = iota_u == jnp.where(u >= low.astype(F32), u - start.astype(F32), -1.0).astype(BF)
    parts = [jnp.where(mask, values[c:c + 1].astype(BF), zero) for c in range(4)] + [jnp.where(mask, one, zero)]
    hot = jnp.where(iota_l == l.astype(BF), one, zero)
    sums = lax.dot_general(jnp.concatenate(parts, axis=0), hot, NTD, preferred_element_type=F32)
    for c in range(5):
        acc_ref[c, pl.ds(start, window), :] += sums[window * c:window * c + window]


def spread(pair_ref, val_ref, code_ref):
    lane = lax.broadcasted_iota(jnp.int32, (8, 128), 1)
    first, last = jnp.zeros((8, 128), F32), jnp.zeros((8, 128), F32)
    lows, highs = [None] * 3, [None] * 3
    for half in range(2):
        for g in range(8):
            at = 128 * (8 * half + g)
            vals = pair_ref[half, g, 0:48, :].astype(F32)
            codes = pair_ref[half, g, 48:72, :].astype(F32)
            for cg in range(3):
                code = codes[8 * cg:8 * cg + 8]
                val_ref[cg, :, at:at + 128] = vals[16 * cg:16 * cg + 16]
                code_ref[cg, :, at:at + 128] = code
                low = jnp.where(code < 1.0, 999.0, code)
                lows[cg] = low if lows[cg] is None else jnp.minimum(lows[cg], low)
                highs[cg] = code if highs[cg] is None else jnp.maximum(highs[cg], code)
    for cg in range(3):
        first = jnp.where(lane == cg, jnp.min(lows[cg], axis=1, keepdims=True) - 1.0, first)
        last = jnp.where(lane == cg, jnp.max(highs[cg], axis=1, keepdims=True) - 1.0, last)
    return first.astype(jnp.int32), last.astype(jnp.int32)


def split(x):
    hi = x.astype(BF)
    return hi, (x - hi.astype(F32)).astype(BF)


def quad(a, b, c, d):
    return jnp.concatenate([jnp.concatenate([a, b], axis=1), jnp.concatenate([c, d], axis=1)], axis=0)


def swap(x):
    return quad(x[:256, :256], x[256:, :256], x[:256, 256:], x[256:, 256:])


def fit(acc_ref, w_ref, tab_ref, out_hbm, out_ref, out_sem):
    kr, ki = tab_ref[0].astype(BF), tab_ref[1].astype(BF)
    plain, conj = quad(kr, -ki, ki, kr), quad(kr, ki, -ki, kr)
    dot = functools.partial(jnp.dot, preferred_element_type=F32)

    def left(x, m):
        return dot(jnp.concatenate([m, m], axis=1), jnp.concatenate(split(x), axis=0))

    def right(x, m):
        return dot(jnp.concatenate(split(x), axis=1), jnp.concatenate([m, m], axis=0))

    def forward(x):
        return swap(right(swap(left(x, plain)), conj))

    def inverse(x):
        return swap(right(swap(left(x, conj)), plain))

    def plane(f):
        return jnp.concatenate([w_ref[pl.ds(2 * h + f, 256, stride=4), :] for h in range(2)], axis=1)

    w0, w1 = plane(0) * TABLE_SCALE, plane(1) * TABLE_SCALE
    w = quad(w0, w1, w0, w1)
    lane = lax.broadcasted_iota(jnp.int32, (1, 512), 1)

    def total(x):
        s = jnp.sum(x, axis=0, keepdims=True)
        a = jnp.sum(s[:, :256], axis=1, keepdims=True)
        b = jnp.sum(s[:, 256:], axis=1, keepdims=True)
        return jnp.where(lane < 256, a, b)

    hits = acc_ref[4]
    hits = quad(hits, hits, hits, hits)
    field = quad(acc_ref[0], acc_ref[1], acc_ref[2], acc_ref[3])
    residual = w * swap(right(swap(dot(plain, field.astype(BF))), conj))
    norm = total(residual * residual)
    g0 = inverse(w * residual)
    pulled = hits * g0
    alpha = norm / (total(pulled * g0) + DAMPING * norm + EPS)
    direction = residual
    residual = residual - alpha * (w * forward(pulled) + DAMPING * direction)
    new = total(residual * residual)
    direction = residual + (new / (norm + EPS)) * direction
    g1 = swap(dot(swap(dot(conj, (w * direction).astype(BF))).astype(BF), plain))
    beta = new / (total(hits * g1 * g1) + DAMPING * total(direction * direction) + EPS)
    stores = [pltpu.make_async_copy(out_ref.at[part], out_hbm.at[part], out_sem.at[part]) for part in range(2)]
    for part in range(2):
        rows = slice(256 * part, 256 * part + 256)
        model = alpha * g0[rows] + beta * g1[rows]
        for f in range(2):
            for h in range(2):
                at = 256 * f + 128 * h
                out_ref[part, pl.ds(2 * h + f, 256, stride=4), :] = model[:, at:at + 128]
        stores[part].start()
    for store in stores:
        store.wait()


def solve_kernel(pair_ref, w_hbm, tab_hbm, out_hbm, out_ref, acc_ref, w_ref, tab_ref, val_ref, code_ref, span_vm, span_sm, sems,
                 out_sem):
    fetch = [pltpu.make_async_copy(w_hbm, w_ref, sems.at[0]), pltpu.make_async_copy(tab_hbm, tab_ref, sems.at[1])]
    for copy in fetch:
        copy.start()
    span_vm[0], span_vm[1] = spread(pair_ref, val_ref, code_ref)
    spans = pltpu.make_async_copy(span_vm, span_sm, sems.at[2])
    spans.start()
    acc_ref[...] = jnp.zeros_like(acc_ref)
    spans.wait()

    for cg in range(3):
        steps, usual = [], True
        for i in range(4):
            first, last = span_sm[0, i, cg], span_sm[1, i, cg]
            first = jnp.minimum((first // 8) * 8, 248)
            wide = last - first
            usual = jnp.logical_and(usual, wide < USUAL[cg][i])
            steps.append((first, sum((wide >= WINDOW * k).astype(jnp.int32) for k in range(-(-256 // WINDOW)))))

        def add(i, low, window):
            code = code_ref[cg]
            bin_step(val_ref[cg, 4 * i:4 * i + 4, :], code[i:i + 1] - 1.0, code[4 + i:5 + i], low, window, acc_ref)

        @pl.when(usual)
        def _():
            for i in range(4):
                add(i, steps[i][0], USUAL[cg][i])

        @pl.when(jnp.logical_not(usual))
        def _():
            for i in range(4):
                pl.loop(0, steps[i][1])(lambda again: add(i, steps[i][0] + again * WINDOW, WINDOW))

    for copy in fetch:
        copy.wait()
    fit(acc_ref, w_ref, tab_ref, out_hbm, out_ref, out_sem)


MESH_ID = pl.DeviceIdType.MESH


def peer_loop(n, me, body):
    lax.fori_loop(1, n, lambda i, carry: (body(lax.rem(me + i, n)), carry)[1], 0)


def exchange_kernel(bins_ref, traces_ref, route_ref, cell_ref, out_ref,
                    traces_vm, hot_vm, bins_vm, msg_out, msg_in, pair_out,
                    trace_sem, own_sem, bin_send, bin_recv, msg_send, msg_recv, pair_send, pair_recv):
    me_p, me_f = lax.axis_index("patch"), lax.axis_index("freq")
    me_x, me_z = me_p // 8, lax.rem(me_p, 8)
    barrier = pltpu.get_barrier_semaphore()
    peer_loop(8, me_f, lambda f: pl.semaphore_signal(barrier, inc=1, device_id={"freq": f}, device_id_type=MESH_ID))
    peer_loop(32, me_p, lambda p: pl.semaphore_signal(barrier, inc=1, device_id={"patch": p}, device_id_type=MESH_ID))
    fetch = pltpu.make_async_copy(traces_ref, traces_vm, trace_sem)
    fetch.start()
    sub = lax.broadcasted_iota(jnp.int32, (8, 128), 0)
    bins_vm[me_f] = jnp.where((sub & 1) == 1, bins_ref[1], bins_ref[0])

    def bin_copy(f, slot):
        return pltpu.make_async_remote_copy(
            src_ref=bins_vm.at[me_f], dst_ref=bins_vm.at[slot], send_sem=bin_send.at[f],
            recv_sem=bin_recv.at[slot], device_id={"freq": f}, device_id_type=MESH_ID)

    def msg_copy(p, slot):
        return pltpu.make_async_remote_copy(
            src_ref=msg_out.at[p], dst_ref=msg_in.at[slot], send_sem=msg_send.at[p],
            recv_sem=msg_recv.at[slot], device_id={"patch": p}, device_id_type=MESH_ID)

    def pair_copy(half, f, slot):
        return pltpu.make_async_remote_copy(
            src_ref=pair_out.at[half, f], dst_ref=out_ref.at[half, slot], send_sem=pair_send.at[half, f],
            recv_sem=pair_recv.at[half, slot], device_id={"freq": f}, device_id_type=MESH_ID)

    def own_copy(half):
        return pltpu.make_async_copy(pair_out.at[half, me_f], out_ref.at[half, me_f], own_sem.at[half])

    pl.semaphore_wait(barrier, 38)
    peer_loop(8, me_f, lambda f: bin_copy(f, me_f).start())
    key, third = routing(route_ref[...], cell_ref[...])
    hot_vm[...] = one_hot_rows(key)
    peer_loop(8, me_f, lambda f: bin_copy(f, f).wait_recv())
    basis = make_basis(bins_vm, traces_vm.shape[1])
    fetch.wait()
    spectra = lax.dot_general(basis, traces_vm[...], NTD, preferred_element_type=F32)
    stacked = stack_rows(spectra, third, cell_ref[...])
    order = [(dx, dz) for dx in (1, 2, 3, 0) for dz in (4, 3, 5, 2, 6, 1, 7, 0)]
    targets = [lax.rem(me_x + dx, 4) * 8 + lax.rem(me_z + dz, 8) for dx, dz in order]
    sources = [lax.rem(me_x + 4 - dx, 4) * 8 + lax.rem(me_z + 8 - dz, 8) for dx, dz in order]
    for k in range(4):
        plane = lax.rem(me_x + order[8 * k][0], 4)
        packed = lax.dot_general(stacked, hot_vm[pl.ds(pl.multiple_of(256 * plane, 256), 256), :], NTD, preferred_element_type=F32)
        write_messages(packed, 8 * lax.rem(me_p, 16), 8 * plane, msg_out)
        for p in [i for i in range(8 * k, 8 * k + 8) if order[i] != (0, 0)]:
            msg_copy(targets[p], me_p).start()
    msg_in[me_p] = msg_out[me_p]
    for half in range(2):
        for i in range(16 * half, 16 * half + 16):
            if order[i] != (0, 0):
                msg_copy(sources[i], sources[i]).wait_recv()
        first = lax.rem(me_x + 4 - order[16 * half][0], 4)
        second = lax.rem(me_x + 4 - order[16 * half + 8][0], 4)
        is_odd = lax.rem(first, 2)
        planes = (first + is_odd * (second - first), second + is_odd * (first - second))
        regroup(msg_in, [planes[t // 8] * 8 + t % 8 for t in range(16)], pair_out.at[half])
        peer_loop(8, me_f, lambda f: pair_copy(half, f, me_f).start())
        own_copy(half).start()
    peer_loop(8, me_f, lambda f: bin_copy(f, me_f).wait_send())
    for i in range(32):
        if order[i] != (0, 0):
            msg_copy(targets[i], me_p).wait_send()
    for half in range(2):
        own_copy(half).wait()
        peer_loop(8, me_f, lambda f: pair_copy(half, f, f).wait_recv())
        peer_loop(8, me_f, lambda f: pair_copy(half, f, me_f).wait_send())

def on_device(traces, routes, cells, band_bins, spectral_weight):
    rows = traces.shape[0]
    vm = pl.BlockSpec(memory_space=pltpu.VMEM)
    sm = pl.BlockSpec(memory_space=pltpu.SMEM)
    anywhere = pl.BlockSpec(memory_space=pl.ANY)
    dma = pltpu.SemaphoreType.DMA
    both = pl.pallas_call(
        exchange_kernel,
        out_shape=jax.ShapeDtypeStruct((2, 8, 72, 128), BF),
        in_specs=[sm, anywhere, vm, vm],
        out_specs=anywhere,
        scratch_shapes=[
            pltpu.VMEM(traces.shape, BF), pltpu.VMEM((1024, rows), BF), pltpu.VMEM((8, 8, 128), jnp.int32),
            pltpu.VMEM((32, 32, 128), BF), pltpu.VMEM((32, 32, 128), BF), pltpu.VMEM((2, 8, 72, 128), BF),
            dma, dma((2,)), dma((8,)), dma((8,)), dma((32,)), dma((32,)), dma((2, 8)), dma((2, 8)),
        ],
        compiler_params=pltpu.CompilerParams(
            collective_id=0, has_side_effects=True, vmem_limit_bytes=62 * 1024 * 1024),
        name="exchange",
    )(band_bins, traces, routes.reshape(1, rows), cells.reshape(1, rows))
    weight = spectral_weight.reshape(2, 512, 128).transpose(1, 0, 2).reshape(1024, 128)
    out = pl.pallas_call(
        solve_kernel,
        out_shape=jax.ShapeDtypeStruct((2, 1024, 128), F32),
        in_specs=[vm, anywhere, anywhere], out_specs=anywhere,
        scratch_shapes=[
            pltpu.VMEM((2, 1024, 128), F32), pltpu.VMEM((5, 256, 256), F32), pltpu.VMEM((1024, 128), F32), pltpu.VMEM((2, 256, 256), F32),
            pltpu.VMEM((3, 16, 2048), F32), pltpu.VMEM((3, 8, 2048), F32),
            pltpu.VMEM((2, 8, 128), jnp.int32), pltpu.SMEM((2, 8, 128), jnp.int32), dma((3,)), dma((2,)),
        ],
        compiler_params=pltpu.CompilerParams(vmem_limit_bytes=60 * 1024 * 1024),
        name="solve",
    )(both, weight, jnp.asarray(kernel_table()))
    return out.reshape(2, 512, 2, 128).transpose(0, 2, 1, 3).reshape(2, 2, 65536)


def solution(mesh):
    return jax.shard_map(
        on_device,
        mesh=mesh,
        in_specs=(P(("patch", "freq"), None), P(("patch", "freq"), None), P(("patch", "freq")), P("freq"), P("freq", "patch")),
        out_specs=P(None, "freq", "patch"),
        check_vma=False,
    )
```
